32 devices in a mesh: group: 2 (over x), tensor: 16 (over z, y, core).
Axes of the slice: x: 2, y: 2, z: 4, core: 2. Of those that a mesh axis runs over, the one named last changes fastest.
Arguments:
- three_center: bfloat16 [32, 8, 4096, 128], P(('group', 'tensor')), parts along dimension 0, may hold values from -0.1875 to 0.1875
- occ_green: bfloat16 [16, 512, 512], P('tensor'), may hold values from -0.25 to 0.25
- virt_green: bfloat16 [16, 512, 512], P('tensor'), may hold values from -0.25 to 0.25
- neighbors: int32 [16, 8], replicated, may hold values from -1 to 15, as said below
Outputs:
- polarization: float32 [256, 128], P(('group', 'tensor')), parts along dimension 0
The draws below stay inside these ranges and needn't reach their ends.
There are 2 independent parts, one for each index of `group`. The reference program is written for one: setup_inputs(seed, part) draws one part's arguments, and reference() takes and returns one part's arrays. A program takes and returns all parts, laid end to end along the dimension named above; an argument that names none is the same for every part. Nothing has to cross between parts.
Inputs may be any that keep to these rules, and one draw needn't show every extreme that they name: neighbors[a, k] is either -1 (an empty slot) or the molecule a XOR k; neighbors[a, 0] = a; whenever neighbors[a, k] = b >= 0, also neighbors[b, k] = a; some molecule has all 8 slots filled.
All inputs are finite; a program needn't handle non-finite values.
Results may differ from the reference program's by a relative error of at most 0.0041.
Values may be sent and summed in bfloat16 or wider, within the bound.
No kernel may reach another device: no remote copies, remote signals or barrier semaphores. Data moves between devices by JAX's collectives and lax.ppermute only.
A program may use at most 128 MiB of HBM per device.

```python
import jax
import jax.numpy as jnp
from jax import lax

BW = 64
RI = 128
K = 8
NA = 16


def draw_neighbors(key, part):
    key = jax.random.fold_in(key, 7)
    slot_index = jnp.arange(K, dtype=jnp.int32)
    molecule = jnp.arange(NA, dtype=jnp.int32)
    partner = jnp.bitwise_xor(molecule[:, None], slot_index[None, :])
    lower = jnp.minimum(molecule[:, None], partner)
    coins = jax.random.randint(key, (K, NA), 0, 5)
    keep = coins[slot_index[None, :], lower] < 3
    keep = keep | (slot_index[None, :] == 0) | (lower == 0)
    return jnp.where(keep, partner, -1).astype(jnp.int32)


def block_scale(rng, extent, shards, low, high):
    loudness = 1.0
    for axis_at, shards_of in shards:
        steps = jax.random.uniform(jax.random.fold_in(jax.random.fold_in(rng, 6), axis_at), (shards_of,), jnp.float32, low / len(shards), high / len(shards))
        loudness = loudness * jnp.repeat(jnp.exp(steps), extent[axis_at] // shards_of).reshape((-1,) + (1,) * (len(extent) - 1 - axis_at))
    return loudness


def normal_values(rng, shape, deviation, reach, cuts=(), kind=jnp.bfloat16):
    values = jax.random.normal(rng, shape, jnp.float32) * deviation
    if len(cuts) > 0:
        values = block_scale(rng, shape, cuts, -0.22, 0.18) * values
    return jnp.clip(values, min=-reach, max=reach).astype(kind)


def setup_inputs(seed: int = 0, part: int = 0) -> dict:
    keys = jax.random.split(jax.random.key(seed), 5)
    part_splits = jax.random.split(jax.random.fold_in(keys[4], part), 5)
    three_center = normal_values(part_splits[0], (NA, K, BW * BW, RI), (2 * K * BW) ** -0.5, 0.1875, ((0, 16),))
    occ_green = normal_values(keys[1], (NA, K * BW, K * BW), (K * BW) ** -0.5, 0.25, ((0, 16),))
    virt_green = normal_values(keys[2], (NA, K * BW, K * BW), (K * BW) ** -0.5, 0.25, ((0, 16),))
    neighbors = draw_neighbors(jax.random.fold_in(keys[4], 71), part)
    return {"three_center": three_center, "occ_green": occ_green, "virt_green": virt_green, "neighbors": neighbors}


def reference(three_center, occ_green, virt_green, neighbors):
    live_slots = neighbors >= 0
    blocks = jnp.where(live_slots[:, :, None, None], three_center, jnp.zeros((), three_center.dtype))
    blocks = blocks.reshape(NA, K, BW, BW, RI)
    occ_all = occ_green.reshape(NA, K, BW, K, BW)
    virt_all = virt_green.reshape(NA, K, BW, K, BW)

    def project(operands):
        occ_one, block_one = operands
        return jnp.einsum("mxny,nzyq->mxzq", occ_one.astype(jnp.float32), block_one.astype(jnp.float32)).astype(jnp.bfloat16)

    projected = lax.map(project, (occ_all, blocks))
    source = jnp.where(live_slots, neighbors, 0).astype(jnp.int32)
    slot_index = jnp.arange(K, dtype=jnp.int32)

    def accumulate(running, operands):
        block_one, virt_one, source_one, live_one = operands
        products = jnp.einsum("milp,mlkj->kijp", block_one.astype(jnp.float32), virt_one.astype(jnp.float32)).astype(jnp.bfloat16)
        partner = projected[source_one, slot_index]
        partner = jnp.where(live_one[:, None, None, None], partner, jnp.zeros((), jnp.bfloat16))
        term = jnp.einsum("kijp,kijq->pq", products.astype(jnp.float32), partner.astype(jnp.float32))
        return running + term, None

    polarization, unused = lax.scan(accumulate, jnp.zeros((RI, RI), jnp.float32), (blocks, virt_all, source, live_slots))
    return polarization
```

```python
import functools

import jax
import jax.numpy as jnp
from jax import lax
from jax.experimental import pallas as pl
from jax.experimental.pallas import tpu as pltpu
from jax.sharding import PartitionSpec as P

SLOTS = 8
BF = jnp.bfloat16
F32 = jnp.float32


def gathered_rows(block_ref, first, count, width):
    columns = []
    for step in range(count):
        at = (first + step) * width
        columns.append(jnp.concatenate([block_ref[0, m, at : at + width, :] for m in range(SLOTS)], axis=0))
    return jnp.concatenate(columns, axis=1)


def product_kernel(slots, width, rows, me_ref, neighbors_ref, virt_ref, block_ref, *refs):
    outs, virt_t = refs[:-1], refs[-1]
    me = me_ref[0]
    low, count = slots[0], len(slots)

    @pl.when(pl.program_id(0) == 0)
    def _():
        parts = []
        for m in range(SLOTS):
            part = virt_ref[0, m * width : (m + 1) * width, low * width : (low + count) * width].astype(F32)
            parts.append(jnp.where(neighbors_ref[me, m] >= 0, part, 0.0))
        turned = jnp.concatenate(parts, axis=0).T
        for at, k in enumerate(slots):
            live = neighbors_ref[me, k] >= 0
            virt_t[at * width : (at + 1) * width, :] = jnp.where(
                live, turned[at * width : (at + 1) * width, :], 0.0
            ).astype(BF)

    ri = block_ref.shape[-1]
    for pair in range(rows // 2):
        right = gathered_rows(block_ref, 2 * pair, 2, width)
        both = jnp.dot(virt_t[...], right, preferred_element_type=F32).astype(BF)
        for at in range(count):
            for half in range(2):
                row = (2 * pair + half) * width
                outs[at][row : row + width, :] = both[at * width : (at + 1) * width, half * ri : (half + 1) * ri]


def products(slots, me, neighbors, virt, blocks, rows=8):
    pairs, ri = blocks.shape[2:]
    wide = virt.shape[1]
    width = wide // SLOTS
    steps = width // rows
    chunk = rows * width
    return pl.pallas_call(
        functools.partial(product_kernel, slots, width, rows),
        grid=(steps,),
        in_specs=[
            pl.BlockSpec(memory_space=pltpu.SMEM),
            pl.BlockSpec(memory_space=pltpu.SMEM),
            pl.BlockSpec((1, wide, wide), lambda s: (0, 0, 0)),
            pl.BlockSpec((1, SLOTS, chunk, ri), lambda s: (0, 0, s, 0)),
        ],
        out_specs=[pl.BlockSpec((chunk, ri), lambda s: (s, 0))] * len(slots),
        out_shape=[jax.ShapeDtypeStruct((pairs, ri), BF)] * len(slots),
        scratch_shapes=[pltpu.VMEM((len(slots) * width, wide), BF)],
        compiler_params=pltpu.CompilerParams(vmem_limit_bytes=32 << 20),
        cost_estimate=pl.CostEstimate(
            flops=2 * len(slots) * width * wide * width * ri,
            bytes_accessed=2 * (SLOTS + len(slots)) * pairs * ri,
            transcendentals=0,
        ),
        name="products",
    )(me, neighbors, virt, blocks)


def project_kernel(width, rows, me_ref, neighbors_ref, occ_ref, block_ref, *refs):
    outs, occ, turn = refs[:-2], refs[-2], refs[-1]
    me = me_ref[0]
    wide = SLOTS * width

    @pl.when(pl.program_id(0) == 0)
    def _():
        lane = lax.broadcasted_iota(jnp.int32, (1, wide), 1) // width
        keep = jnp.zeros((1, wide), F32)
        for n in range(SLOTS):
            keep = jnp.where((lane == n) & (neighbors_ref[me, n] >= 0), 1.0, keep)
        occ[...] = (occ_ref[0].astype(F32) * keep).astype(BF)

    ri = block_ref.shape[-1]
    for pair in range(rows // 2):
        right = gathered_rows(block_ref, 2 * pair, 2, width)
        both = jnp.dot(occ[...], right, preferred_element_type=F32)
        for half in range(2):
            turn[pl.ds(2 * pair + half, wide, stride=rows), :] = both[:, half * ri : (half + 1) * ri]
    for m in range(SLOTS):
        piece = turn[m * width * rows : (m + 1) * width * rows, :]
        outs[m][...] = piece.astype(BF).reshape(width, rows, ri)


def projections(me, neighbors, occ, blocks, rows=16):
    pairs, ri = blocks.shape[2:]
    wide = occ.shape[1]
    width = wide // SLOTS
    steps = width // rows
    chunk = rows * width
    out = pl.pallas_call(
        functools.partial(project_kernel, width, rows),
        grid=(steps,),
        in_specs=[
            pl.BlockSpec(memory_space=pltpu.SMEM),
            pl.BlockSpec(memory_space=pltpu.SMEM),
            pl.BlockSpec((1, wide, wide), lambda s: (0, 0, 0)),
            pl.BlockSpec((1, SLOTS, chunk, ri), lambda s: (0, 0, s, 0)),
        ],
        out_specs=[pl.BlockSpec((width, rows, ri), lambda s: (0, s, 0))] * SLOTS,
        out_shape=[jax.ShapeDtypeStruct((width, width, ri), BF)] * SLOTS,
        scratch_shapes=[pltpu.VMEM((wide, wide), BF), pltpu.VMEM((wide * rows, ri), F32)],
        compiler_params=pltpu.CompilerParams(vmem_limit_bytes=40 << 20),
        cost_estimate=pl.CostEstimate(
            flops=2 * wide * wide * width * ri, bytes_accessed=4 * SLOTS * pairs * ri, transcendentals=0
        ),
        name="projections",
    )(me, neighbors, occ, blocks)
    return [each.reshape(pairs, ri) for each in out]


def contract_kernel(count, has_start, *refs):
    lefts, rights = refs[:count], refs[count : 2 * count]
    out = refs[-1]

    @pl.when(pl.program_id(0) == 0)
    def _():
        out[...] = refs[2 * count][...] if has_start else jnp.zeros_like(out)

    total = out[...]
    for left, right in zip(lefts, rights):
        total += lax.dot_general(
            left[...], right[...], (((0,), (0,)), ((), ())), preferred_element_type=F32
        )
    out[...] = total


def contract(lefts, rights, start=None, chunk=1024):
    pairs, ri = lefts[0].shape
    count = len(lefts)
    starts = [] if start is None else [start]
    whole = pl.BlockSpec((ri, ri), lambda s: (0, 0))
    return pl.pallas_call(
        functools.partial(contract_kernel, count, start is not None),
        grid=(pairs // chunk,),
        in_specs=[pl.BlockSpec((chunk, ri), lambda s: (s, 0))] * (2 * count) + [whole] * len(starts),
        out_specs=whole,
        out_shape=jax.ShapeDtypeStruct((ri, ri), F32),
        compiler_params=pltpu.CompilerParams(vmem_limit_bytes=32 << 20),
        cost_estimate=pl.CostEstimate(
            flops=2 * count * pairs * ri * ri, bytes_accessed=4 * count * pairs * ri, transcendentals=0
        ),
        name="contract",
    )(*lefts, *rights, *starts)


def exchange(value, k, devices):
    return lax.ppermute(value, "tensor", [(i, i ^ k) for i in range(devices)])


def reduce_rows(total, devices, order):
    index = lax.axis_index("tensor")
    bits = [1 << b for b in reversed(range(devices.bit_length() - 1))]
    value = total.reshape((2,) * len(bits) + (total.shape[0] // devices, total.shape[1]))
    left = list(bits)
    for k in order:
        at = left.index(k)
        left.pop(at)
        low = lax.index_in_dim(value, 0, at, keepdims=False)
        high = lax.index_in_dim(value, 1, at, keepdims=False)
        upper = (index // k) % 2 == 1
        value = jnp.where(upper, high, low) + exchange(jnp.where(upper, low, high), k, devices)
    return value


def local(devices, three_center, occ_green, virt_green, neighbors):
    me = lax.axis_index("tensor").astype(jnp.int32).reshape(1)
    sides = {}
    sides[6], sides[7] = products((6, 7), me, neighbors, virt_green, three_center)
    arrived = {k: exchange(sides[k], k, devices) for k in (6, 7)}
    early = (0, 1, 2, 3, 4, 5)
    for k, value in zip(early, products(early, me, neighbors, virt_green, three_center)):
        sides[k] = value
    for k in (2, 4, 3, 5, 1):
        arrived[k] = exchange(sides[k], k, devices)
    arrived[0] = sides[0]
    project = projections(me, neighbors, occ_green, three_center)
    order = (0, 1, 6, 7, 2, 4, 3, 5)
    groups = ((0, 1), (6, 7), (2, 4), (3, 5))
    total = None
    for group in groups:
        total = contract([arrived[k] for k in group], [project[k] for k in group], total)
    bits = [1 << b for b in reversed(range(devices.bit_length() - 1))]
    return reduce_rows(total, devices, bits)


def solution(mesh):
    devices = mesh.shape["tensor"]
    in_specs = (
        P(("group", "tensor"), None, None, None),
        P("tensor", None, None),
        P("tensor", None, None),
        P(),
    )
    out_specs = P(("group", "tensor"), None)
    return jax.shard_map(
        functools.partial(local, devices), mesh=mesh, in_specs=in_specs, out_specs=out_specs, check_vma=False
    )
```

```python
import functools

import jax
import jax.numpy as jnp
from jax import lax
from jax.experimental import pallas as pl
from jax.experimental.pallas import tpu as pltpu
from jax.sharding import PartitionSpec as P

SLOTS = 8
BF = jnp.bfloat16
F32 = jnp.float32


def gathered_rows(block, first, count, width):
    columns = []
    for step in range(count):
        rows = pl.ds(pl.multiple_of(first + step * width, width), width)
        columns.append(jnp.concatenate([block[m, rows, :] for m in range(SLOTS)], axis=0))
    return jnp.concatenate(columns, axis=1)


def product_kernel(slots, width, chunks, me_ref, neighbors_ref, virt_hbm, block_hbm, *refs):
    outs = refs[-5 - len(slots) : -5]
    virt, virt_t, block, virt_sem, sems = refs[-5:]
    me = me_ref[0]
    low, count = slots[0], len(slots)
    ri = block.shape[-1]
    size = block.shape[1] // chunks

    def block_copy(c):
        rows = pl.ds(pl.multiple_of(c * size, size), size)
        return pltpu.make_async_copy(block_hbm.at[0, :, rows, :], block.at[:, rows, :], sems.at[c])

    virt_copy = pltpu.make_async_copy(
        virt_hbm.at[0, :, pl.ds(low * width, count * width)], virt, virt_sem
    )
    virt_copy.start()
    for c in range(chunks):
        block_copy(c).start()
    virt_copy.wait()
    parts = [
        jnp.where(neighbors_ref[m, me] >= 0, virt[m * width : (m + 1) * width, :].astype(F32), 0.0)
        for m in range(SLOTS)
    ]
    turned = jnp.concatenate(parts, axis=0).T
    for at, k in enumerate(slots):
        live = neighbors_ref[k, me] >= 0
        virt_t[at * width : (at + 1) * width, :] = jnp.where(
            live, turned[at * width : (at + 1) * width, :], 0.0
        ).astype(BF)

    @pl.loop(0, chunks)
    def _(c):
        block_copy(c).wait()
        for pair in range(size // width // 2):
            base = c * size + 2 * pair * width
            right = gathered_rows(block, base, 2, width)
            both = jnp.dot(virt_t[...], right, preferred_element_type=F32).astype(BF)
            for at in range(count):
                for half in range(2):
                    rows = pl.ds(pl.multiple_of(base + half * width, width), width)
                    outs[at][rows, :] = both[at * width : (at + 1) * width, half * ri : (half + 1) * ri]


def products(slots, me, neighbors, virt, blocks, chunks, after=None, near=False):
    pairs, ri = blocks.shape[2:]
    wide = virt.shape[1]
    width = wide // SLOTS
    count = len(slots)
    smem = pl.BlockSpec(memory_space=pltpu.SMEM)
    hbm = pl.BlockSpec(memory_space=pltpu.HBM)
    after = [] if after is None else [after]
    return pl.pallas_call(
        functools.partial(product_kernel, slots, width, chunks),
        in_specs=[smem, smem, hbm, hbm] + [pl.BlockSpec(memory_space=pl.ANY)] * len(after),
        out_specs=[pl.BlockSpec(memory_space=pltpu.VMEM)] * count,
        out_shape=[pltpu.VMEM((pairs, ri), BF) if near else pltpu.HBM((pairs, ri), BF)] * count,
        scratch_shapes=[
            pltpu.VMEM((wide, count * width), BF),
            pltpu.VMEM((count * width, wide), BF),
            pltpu.VMEM((SLOTS, pairs, ri), BF),
            pltpu.SemaphoreType.DMA,
            pltpu.SemaphoreType.DMA((chunks,)),
        ],
        compiler_params=pltpu.CompilerParams(vmem_limit_bytes=24 << 20),
        cost_estimate=pl.CostEstimate(flops=1, bytes_accessed=1, transcendentals=0),
        name="products",
    )(me, neighbors, virt, blocks, *after)


def project_kernel(width, rows, me_ref, neighbors_ref, occ_ref, block_ref, *refs):
    outs, occ, turn = refs[:-2], refs[-2], refs[-1]
    me = me_ref[0]
    wide = SLOTS * width

    @pl.when(pl.program_id(0) == 0)
    def _():
        slot = lax.broadcasted_iota(jnp.int32, (1, wide), 1) // width
        keep = jnp.zeros((1, wide), F32)
        for n in range(SLOTS):
            keep = jnp.where((slot == n) & (neighbors_ref[n, me] >= 0), 1.0, keep)
        occ[...] = (occ_ref[0].astype(F32) * keep).astype(BF)

    ri = block_ref.shape[-1]
    for pair in range(rows // 2):
        right = gathered_rows(block_ref.at[0], 2 * pair * width, 2, width)
        both = jnp.dot(occ[...], right, preferred_element_type=F32)
        for half in range(2):
            turn[pl.ds(2 * pair + half, wide, stride=rows), :] = both[:, half * ri : (half + 1) * ri]
    for m in range(SLOTS):
        piece = turn[m * width * rows : (m + 1) * width * rows, :]
        outs[m][...] = piece.astype(BF).reshape(width, rows, ri)


def projections(me, neighbors, occ, blocks, rows=16):
    pairs, ri = blocks.shape[2:]
    wide = occ.shape[1]
    width = wide // SLOTS
    steps = width // rows
    chunk = rows * width
    smem = pl.BlockSpec(memory_space=pltpu.SMEM)
    out = pl.pallas_call(
        functools.partial(project_kernel, width, rows),
        grid=(steps,),
        in_specs=[
            smem,
            smem,
            pl.BlockSpec((1, wide, wide), lambda s: (0, 0, 0)),
            pl.BlockSpec((1, SLOTS, chunk, ri), lambda s: (0, 0, s, 0)),
        ],
        out_specs=[pl.BlockSpec((width, rows, ri), lambda s: (0, s, 0))] * SLOTS,
        out_shape=[pltpu.HBM((width, width, ri), BF)] * SLOTS,
        scratch_shapes=[pltpu.VMEM((wide, wide), BF), pltpu.VMEM((wide * rows, ri), F32)],
        compiler_params=pltpu.CompilerParams(vmem_limit_bytes=20 << 20),
        cost_estimate=pl.CostEstimate(flops=1, bytes_accessed=1, transcendentals=0),
        name="projections",
    )(me, neighbors, occ, blocks)
    return [each.reshape(pairs, ri) for each in out]


def turn_kernel(count, *refs):
    span = refs[0].shape[1]
    for source, out in zip(refs[:count], refs[count:]):

        @pl.loop(0, source.shape[0] // span)
        def _(c):
            at = pl.ds(pl.multiple_of(c * span, span), span)
            out[:, at] = source[at, :].T


def turned(values):
    pairs, ri = values[0].shape
    vmem = pl.BlockSpec(memory_space=pltpu.VMEM)
    return pl.pallas_call(
        functools.partial(turn_kernel, len(values)),
        in_specs=[vmem] * len(values),
        out_specs=[vmem] * len(values),
        out_shape=[pltpu.VMEM((ri, pairs), BF)] * len(values),
        compiler_params=pltpu.CompilerParams(vmem_limit_bytes=12 << 20),
        cost_estimate=pl.CostEstimate(flops=1, bytes_accessed=1, transcendentals=0),
        name="turn",
    )(*values)


def contract_kernel(count, has_start, last, *refs):
    lefts, rights = refs[:count], refs[count : 2 * count]
    out = refs[-1]
    total = refs[2 * count][...] if has_start else None
    for left, right in zip(lefts, rights):
        dims = (((1 if last else 0,), (0,)), ((), ()))
        term = lax.dot_general(left[...], right[...], dims, preferred_element_type=F32)
        total = term if total is None else total + term
    out[...] = total.T if last else total


def contract(lefts, rights, start=None, last=False):
    ri = rights[0].shape[1]
    count = len(lefts)
    starts = [] if start is None else [start]
    vmem = pl.BlockSpec(memory_space=pltpu.VMEM)
    return pl.pallas_call(
        functools.partial(contract_kernel, count, start is not None, last),
        in_specs=[vmem] * (2 * count + len(starts)),
        out_specs=vmem,
        out_shape=pltpu.VMEM((ri, ri), F32),
        compiler_params=pltpu.CompilerParams(vmem_limit_bytes=12 << 20),
        cost_estimate=pl.CostEstimate(flops=1, bytes_accessed=1, transcendentals=0),
        name="contract",
    )(*lefts, *rights, *starts)


def exchange(value, k, devices):
    return lax.ppermute(value, "tensor", [(i, i ^ k) for i in range(devices)])


def reduce_rows(total, devices, order):
    index = lax.axis_index("tensor")
    bits = [1 << b for b in reversed(range(devices.bit_length() - 1))]
    value = total.reshape((2,) * len(bits) + (total.shape[0] // devices, total.shape[1]))
    left = list(bits)
    for k in order:
        at = left.index(k)
        left.pop(at)
        low = lax.index_in_dim(value, 0, at, keepdims=False)
        high = lax.index_in_dim(value, 1, at, keepdims=False)
        upper = (index & k) != 0
        value = jnp.where(upper, high, low) + exchange(jnp.where(upper, low, high), k, devices)
    return value


def local(devices, three_center, occ_green, virt_green, neighbors):
    me = lax.axis_index("tensor").astype(jnp.int32).reshape(1)
    by_slot = pltpu.with_memory_space_constraint(neighbors.T, pltpu.HBM)
    three_center = pltpu.with_memory_space_constraint(three_center, pltpu.HBM)
    occ_green = pltpu.with_memory_space_constraint(occ_green, pltpu.HBM)
    virt_green = pltpu.with_memory_space_constraint(virt_green, pltpu.HBM)
    sides = dict(zip((6, 7), products((6, 7), me, by_slot, virt_green, three_center, 2, near=True)))
    arrived = {k: exchange(sides[k], k, devices) for k in (6, 7)}
    middle = (2, 3, 4, 5)
    sides.update(zip(middle, products(middle, me, by_slot, virt_green, three_center, 4, sides[6])))
    for k in (2, 4, 3, 5):
        arrived[k] = exchange(sides[k], k, devices)
    sides.update(zip((0, 1), products((0, 1), me, by_slot, virt_green, three_center, 2, arrived[6])))
    arrived[0] = sides[0]
    arrived[1] = exchange(sides[1], 1, devices)
    project = projections(me, by_slot, occ_green, three_center)
    project[3], project[5] = turned((project[3], project[5]))
    groups = ((6,), (0, 7), (1, 2, 4), (3, 5))
    total = None
    for group in groups:
        total = contract(
            [project[k] for k in group], [arrived[k] for k in group], total, group is groups[-1]
        )
    bits = [1 << b for b in reversed(range(devices.bit_length() - 1))]
    return reduce_rows(total, devices, bits)


def solution(mesh):
    devices = mesh.shape["tensor"]
    in_specs = (
        P(("group", "tensor"), None, None, None),
        P("tensor", None, None),
        P("tensor", None, None),
        P(),
    )
    out_specs = P(("group", "tensor"), None)
    return jax.shard_map(
        functools.partial(local, devices), mesh=mesh, in_specs=in_specs, out_specs=out_specs, check_vma=False
    )
```

```python
import functools

import jax
import jax.numpy as jnp
from jax import lax
from jax.experimental import pallas as pl
from jax.experimental.pallas import tpu as pltpu
from jax.sharding import PartitionSpec as P

SLOTS = 8
BF = jnp.bfloat16
F32 = jnp.float32


def gathered_rows(block, first, count, width):
    columns = []
    for step in range(count):
        rows = pl.ds(pl.multiple_of(first + step * width, width), width)
        columns.append(jnp.concatenate([block[m, rows, :] for m in range(SLOTS)], axis=0))
    return jnp.concatenate(columns, axis=1)


def masked_turned(slots, width, me, neighbors_ref, virt, virt_t):
    parts = [
        jnp.where(neighbors_ref[m, me] >= 0, virt[m * width : (m + 1) * width, :].astype(F32), 0.0)
        for m in range(SLOTS)
    ]
    turned = jnp.concatenate(parts, axis=0).T
    for at, k in enumerate(slots):
        live = neighbors_ref[k, me] >= 0
        virt_t[at * width : (at + 1) * width, :] = jnp.where(
            live, turned[at * width : (at + 1) * width, :], 0.0
        ).astype(BF)


def product_kernel(slots, width, chunks, me_ref, neighbors_ref, virt_hbm, block_hbm, *refs):
    outs = refs[-5 - len(slots) : -5]
    virt, virt_t, block, virt_sem, sems = refs[-5:]
    me = me_ref[0]
    low, count = slots[0], len(slots)
    ri = block.shape[-1]
    size = block.shape[1] // chunks

    def block_copy(c):
        rows = pl.ds(pl.multiple_of(c * size, size), size)
        return pltpu.make_async_copy(block_hbm.at[0, :, rows, :], block.at[:, rows, :], sems.at[c])

    virt_copy = pltpu.make_async_copy(
        virt_hbm.at[0, :, pl.ds(low * width, count * width)], virt, virt_sem
    )
    virt_copy.start()
    for c in range(chunks):
        block_copy(c).start()
    virt_copy.wait()
    masked_turned(slots, width, me, neighbors_ref, virt, virt_t)

    @pl.loop(0, chunks)
    def _(c):
        block_copy(c).wait()
        for pair in range(size // width // 2):
            base = c * size + 2 * pair * width
            right = gathered_rows(block, base, 2, width)
            both = jnp.dot(virt_t[...], right, preferred_element_type=F32).astype(BF)
            for at in range(count):
                for half in range(2):
                    rows = pl.ds(pl.multiple_of(base + half * width, width), width)
                    outs[at][rows, :] = both[at * width : (at + 1) * width, half * ri : (half + 1) * ri]


def products(slots, me, neighbors, virt, blocks, chunks, after=None, near=False):
    pairs, ri = blocks.shape[2:]
    wide = virt.shape[1]
    width = wide // SLOTS
    count = len(slots)
    smem = pl.BlockSpec(memory_space=pltpu.SMEM)
    hbm = pl.BlockSpec(memory_space=pltpu.HBM)
    after = [] if after is None else [after]
    return pl.pallas_call(
        functools.partial(product_kernel, slots, width, chunks),
        in_specs=[smem, smem, hbm, hbm] + [pl.BlockSpec(memory_space=pl.ANY)] * len(after),
        out_specs=[pl.BlockSpec(memory_space=pltpu.VMEM)] * count,
        out_shape=[pltpu.VMEM((pairs, ri), BF) if near else pltpu.HBM((pairs, ri), BF)] * count,
        scratch_shapes=[
            pltpu.VMEM((wide, count * width), BF),
            pltpu.VMEM((count * width, wide), BF),
            pltpu.VMEM((SLOTS, pairs, ri), BF),
            pltpu.SemaphoreType.DMA,
            pltpu.SemaphoreType.DMA((chunks,)),
        ],
        compiler_params=pltpu.CompilerParams(vmem_limit_bytes=24 << 20),
        cost_estimate=pl.CostEstimate(flops=1, bytes_accessed=1, transcendentals=0),
        name="products",
    )(me, neighbors, virt, blocks, *after)


def turned_product_kernel(slots, width, chunks, slab, cuts, me_ref, neighbors_ref, virt_hbm, block_hbm, *refs):
    count = len(slots)
    outs = refs[-7 - sum(len(each) for each in cuts) : -7]
    virt, virt_t, block, sides, virt_sem, sems, out_sems = refs[-7:]
    me = me_ref[0]
    low = slots[0]
    ri = block.shape[-1]
    size = block.shape[1] // chunks

    def block_copy(c):
        rows = pl.ds(pl.multiple_of(c * size, size), size)
        return pltpu.make_async_copy(block_hbm.at[0, :, rows, :], block.at[:, rows, :], sems.at[c])

    virt_copy = pltpu.make_async_copy(
        virt_hbm.at[0, :, pl.ds(low * width, count * width)], virt, virt_sem
    )
    virt_copy.start()
    for c in range(chunks):
        block_copy(c).start()
    virt_copy.wait()
    masked_turned(slots, width, me, neighbors_ref, virt, virt_t)

    @pl.loop(0, chunks)
    def _(c):
        block_copy(c).wait()
        for pair in range(size // width // 2):
            base = c * size + 2 * pair * width
            right = gathered_rows(block, base, 2, width)
            both = jnp.dot(virt_t[...], right, preferred_element_type=F32).astype(BF)
            lanes = pl.ds(pl.multiple_of(base, 2 * width), 2 * width)
            for at in range(count):
                mine = both[at * width : (at + 1) * width, :]
                rows = jnp.concatenate([mine[:, :ri], mine[:, ri:]], axis=0)
                sides[at, :, lanes] = rows.T

    copies = []
    outs = list(outs)
    for at, k in enumerate(slots):
        chip = (me ^ k) >> 1
        for first, last in cuts[at]:
            out = outs.pop(0)
            for g in range(first, last):
                source = pl.ds(pl.multiple_of((chip ^ g) * slab, slab), slab)
                target = out.at[pl.ds((g - first) * slab, slab), :]
                copies.append(pltpu.make_async_copy(sides.at[at, source, :], target, out_sems.at[len(copies)]))
    for copy in copies:
        copy.start()
    for copy in copies:
        copy.wait()


def turned_products(slots, me, neighbors, virt, blocks, chunks, slab, cuts, after):
    pairs, ri = blocks.shape[2:]
    wide = virt.shape[1]
    width = wide // SLOTS
    count = len(slots)
    smem = pl.BlockSpec(memory_space=pltpu.SMEM)
    hbm = pl.BlockSpec(memory_space=pltpu.HBM)
    out = pl.pallas_call(
        functools.partial(turned_product_kernel, slots, width, chunks, slab, cuts),
        in_specs=[smem, smem, hbm, hbm, pl.BlockSpec(memory_space=pl.ANY)],
        out_specs=[hbm] * sum(len(each) for each in cuts),
        out_shape=[pltpu.HBM(((last - first) * slab, pairs), BF) for each in cuts for first, last in each],
        scratch_shapes=[
            pltpu.VMEM((wide, count * width), BF),
            pltpu.VMEM((count * width, wide), BF),
            pltpu.VMEM((SLOTS, pairs, ri), BF),
            pltpu.VMEM((count, ri, pairs), BF),
            pltpu.SemaphoreType.DMA,
            pltpu.SemaphoreType.DMA((chunks,)),
            pltpu.SemaphoreType.DMA((count * ri // slab,)),
        ],
        compiler_params=pltpu.CompilerParams(vmem_limit_bytes=24 << 20),
        cost_estimate=pl.CostEstimate(flops=1, bytes_accessed=1, transcendentals=0),
        name="turned_products",
    )(me, neighbors, virt, blocks, after)
    out = list(out)
    return {k: [out.pop(0) for _ in cuts[at]] for at, k in enumerate(slots)}


def project_kernel(width, rows, me_ref, neighbors_ref, occ_ref, block_ref, after_ref, *refs):
    outs, occ, turn = refs[:-2], refs[-2], refs[-1]
    me = me_ref[0]
    wide = SLOTS * width

    @pl.when(pl.program_id(0) == 0)
    def _():
        slot = lax.broadcasted_iota(jnp.int32, (1, wide), 1) // width
        keep = jnp.zeros((1, wide), F32)
        for n in range(SLOTS):
            keep = jnp.where((slot == n) & (neighbors_ref[n, me] >= 0), 1.0, keep)
        occ[...] = (occ_ref[0].astype(F32) * keep).astype(BF)

    ri = block_ref.shape[-1]
    for pair in range(rows // 2):
        right = gathered_rows(block_ref.at[0], 2 * pair * width, 2, width)
        both = jnp.dot(occ[...], right, preferred_element_type=F32)
        for half in range(2):
            turn[pl.ds(2 * pair + half, wide, stride=rows), :] = both[:, half * ri : (half + 1) * ri]
    for m in range(SLOTS):
        piece = turn[m * width * rows : (m + 1) * width * rows, :]
        outs[m][...] = piece.astype(BF).reshape(width, rows, ri)


def projections(me, neighbors, occ, blocks, after, rows=16):
    pairs, ri = blocks.shape[2:]
    wide = occ.shape[1]
    width = wide // SLOTS
    steps = width // rows
    chunk = rows * width
    smem = pl.BlockSpec(memory_space=pltpu.SMEM)
    out = pl.pallas_call(
        functools.partial(project_kernel, width, rows),
        grid=(steps,),
        in_specs=[
            smem,
            smem,
            pl.BlockSpec((1, wide, wide), lambda s: (0, 0, 0)),
            pl.BlockSpec((1, SLOTS, chunk, ri), lambda s: (0, 0, s, 0)),
            pl.BlockSpec(memory_space=pl.ANY),
        ],
        out_specs=[pl.BlockSpec((width, rows, ri), lambda s: (0, s, 0))] * SLOTS,
        out_shape=[(pltpu.VMEM if m in (3, 5) else pltpu.HBM)((width, width, ri), BF) for m in range(SLOTS)],
        scratch_shapes=[pltpu.VMEM((wide, wide), BF), pltpu.VMEM((wide * rows, ri), F32)],
        compiler_params=pltpu.CompilerParams(vmem_limit_bytes=17 << 20),
        cost_estimate=pl.CostEstimate(flops=1, bytes_accessed=1, transcendentals=0),
        name="projections",
    )(me, neighbors, occ, blocks, after)
    return [each.reshape(pairs, ri) for each in out]


def contract_kernel(count, has_start, *refs):
    out = refs[2 * count + has_start + (len(refs) - 2 * count - has_start - 1) // 2]
    total = refs[2 * count][...] if has_start else None
    for left, right in zip(refs[:count], refs[count : 2 * count]):
        term = lax.dot_general(left[...], right[...], (((0,), (0,)), ((), ())), preferred_element_type=F32)
        total = term if total is None else total + term
    out[...] = total


def contract(lefts, rights, start=None, passed=()):
    pairs, ri = rights[0].shape
    count = len(lefts)
    starts = [] if start is None else [start]
    vmem = pl.BlockSpec(memory_space=pltpu.VMEM)
    anywhere = pl.BlockSpec(memory_space=pl.ANY)
    return pl.pallas_call(
        functools.partial(contract_kernel, count, len(starts)),
        in_specs=[vmem] * (2 * count + len(starts)) + [anywhere] * len(passed),
        out_specs=[vmem] + [anywhere] * len(passed),
        out_shape=[pltpu.VMEM((ri, ri), F32)] + [pltpu.HBM(each.shape, each.dtype) for each in passed],
        input_output_aliases={2 * count + len(starts) + at: 1 + at for at in range(len(passed))},
        compiler_params=pltpu.CompilerParams(vmem_limit_bytes=8 << 20),
        cost_estimate=pl.CostEstimate(flops=1, bytes_accessed=1, transcendentals=0),
        name="contract",
    )(*lefts, *rights, *starts, *passed)


def rows_kernel(count, rows, slab, bases, me_ref, *refs):
    lefts, rights = refs[:count], refs[count : 2 * count]
    rest = refs[2 * count : 2 * count + len(bases)]
    passed = (len(refs) - 2 * count - len(bases) - len(rows)) // 2
    outs = refs[2 * count + len(bases) + passed :][: len(rows)]
    chip = me_ref[0] >> 1
    height = sum(rows)
    total = jnp.zeros((height, rights[0].shape[1]), F32)
    for left, right in zip(lefts, rights):
        total += jnp.dot(left[...], right[...], preferred_element_type=F32)
    for base, (kind, first) in zip(rest, bases):
        if kind == "all":
            pieces = []
            for g in range(first, first + height // slab):
                pieces.append(base[pl.ds(pl.multiple_of((chip ^ g) * slab, slab), slab), :])
            total += jnp.concatenate(pieces, axis=0) if len(pieces) > 1 else pieces[0]
        else:
            total += base[...]
    at = 0
    for out, each in zip(outs, rows):
        out[...] = total[at : at + each, :]
        at += each


def contract_rows(me, lefts, rights, rows, slab, bases=(), passed=()):
    ri = rights[0].shape[1]
    count = len(lefts)
    vmem = pl.BlockSpec(memory_space=pltpu.VMEM)
    anywhere = pl.BlockSpec(memory_space=pl.ANY)
    kinds = tuple((kind, first) for kind, first, _ in bases)
    return pl.pallas_call(
        functools.partial(rows_kernel, count, rows, slab, kinds),
        in_specs=[pl.BlockSpec(memory_space=pltpu.SMEM)]
        + [vmem] * (2 * count + len(bases))
        + [anywhere] * len(passed),
        out_specs=[vmem] * len(rows) + [anywhere] * len(passed),
        out_shape=[pltpu.VMEM((each, ri), F32) for each in rows]
        + [pltpu.HBM(each.shape, each.dtype) for each in passed],
        input_output_aliases={1 + 2 * count + len(bases) + at: len(rows) + at for at in range(len(passed))},
        compiler_params=pltpu.CompilerParams(vmem_limit_bytes=8 << 20),
        cost_estimate=pl.CostEstimate(flops=20_000_000_000, bytes_accessed=1, transcendentals=0),
        name="contract_rows",
    )(me, *lefts, *rights, *[array for _, _, array in bases], *passed)


def exchange(value, k, devices):
    return lax.ppermute(value, "tensor", [(i, i ^ k) for i in range(devices)])


def reduce_rows(total, devices, order):
    index = lax.axis_index("tensor")
    bits = [1 << b for b in reversed(range(devices.bit_length() - 1))]
    value = total.reshape((2,) * len(bits) + (total.shape[0] // devices, total.shape[1]))
    left = list(bits)
    for k in order:
        at = left.index(k)
        left.pop(at)
        low = lax.index_in_dim(value, 0, at, keepdims=False)
        high = lax.index_in_dim(value, 1, at, keepdims=False)
        upper = (index & k) != 0
        value = jnp.where(upper, high, low) + exchange(jnp.where(upper, low, high), k, devices)
    return value


def local(devices, three_center, occ_green, virt_green, neighbors):
    me = lax.axis_index("tensor").astype(jnp.int32).reshape(1)
    by_slot = pltpu.with_memory_space_constraint(neighbors.T, pltpu.HBM)
    three_center = pltpu.with_memory_space_constraint(three_center, pltpu.HBM)
    occ_green = pltpu.with_memory_space_constraint(occ_green, pltpu.HBM)
    virt_green = pltpu.with_memory_space_constraint(virt_green, pltpu.HBM)
    sides = dict(zip((6, 7), products((6, 7), me, by_slot, virt_green, three_center, 2, near=True)))
    arrived = {k: exchange(sides[k], k, devices) for k in (6, 7)}
    middle = (2, 3, 4, 5)
    slab = 2 * three_center.shape[-1] // devices
    by_owner = devices == 16 and slab == 16
    if by_owner:
        cuts = (((4, 8), (0, 4)), ((4, 8), (1, 4), (0, 1)), ((4, 8), (0, 4)), ((4, 8), (1, 4), (0, 1)))
        pieces = turned_products(
            middle, me, by_slot, virt_green, three_center, 4, slab, cuts, sides[6]
        )
        latest = pieces[5][0]
    else:
        sides.update(zip(middle, products(middle, me, by_slot, virt_green, three_center, 4, sides[6])))
        for k in middle:
            arrived[k] = exchange(sides[k], k, devices)
        latest = sides[5]
    sides.update(zip((0, 1), products((0, 1), me, by_slot, virt_green, three_center, 2, latest)))
    project = projections(me, by_slot, occ_green, three_center, sides[0])
    arrived[0] = sides[0]
    arrived[1] = exchange(sides[1], 1, devices)
    first, second = (2, 4), (3, 5)
    passed = [pieces[k][0] for k in second] if by_owner else []
    total, *passed = contract([arrived[k] for k in (6, 0)], [project[k] for k in (6, 0)], None, passed)
    if not by_owner:
        for group in ((7, 1), first, second):
            (total,) = contract([arrived[k] for k in group], [project[k] for k in group], total)
        bits = [1 << b for b in reversed(range(devices.bit_length() - 1))]
        return reduce_rows(total, devices, bits)

    def send(values, slots):
        return [exchange(value, k, devices) for k, value in zip(slots, values)]

    first_rights = [project[k] for k in first]
    second_rights = [project[k] for k in second]
    first_far = send([pieces[k][0] for k in first], first)
    second_far = send(passed, second)
    (total,) = contract([arrived[k] for k in (7, 1)], [project[k] for k in (7, 1)], total)
    outer, *passed = contract_rows(
        me, first_far, first_rights, (4 * slab,), slab, [("all", 4, total)], [pieces[k][1] for k in first]
    )
    first_own = send(passed, first)
    outer, *passed = contract_rows(
        me, second_far, second_rights, (4 * slab,), slab, [("own", 0, outer)], [pieces[k][1] for k in second]
    )
    inner = exchange(outer, 8, devices)
    second_mid = send(passed, second)
    chip, rest, *passed = contract_rows(
        me,
        first_own,
        first_rights,
        (slab, 3 * slab),
        slab,
        [("all", 0, total), ("own", 0, inner)],
        [pieces[k][2] for k in second],
    )
    second_near = send(passed, second)
    square = contract_rows(me, second_mid, second_rights, (slab,) * 3, slab, [("own", 0, rest)])
    square = [exchange(value, 2 * (at + 1), devices) for at, value in enumerate(square)]
    (chip,) = contract_rows(me, second_near, second_rights, (slab,), slab, [("own", 0, chip)])
    chip = chip + square[0] + square[1] + square[2]
    half = slab // 2
    upper = (lax.axis_index("tensor") & 1) != 0
    keep = jnp.where(upper, chip[half:], chip[:half])
    return keep + exchange(jnp.where(upper, chip[:half], chip[half:]), 1, devices)


def solution(mesh):
    devices = mesh.shape["tensor"]
    in_specs = (
        P(("group", "tensor"), None, None, None),
        P("tensor", None, None),
        P("tensor", None, None),
        P(),
    )
    out_specs = P(("group", "tensor"), None)
    return jax.shard_map(
        functools.partial(local, devices), mesh=mesh, in_specs=in_specs, out_specs=out_specs, check_vma=False
    )
```

```python
import functools

import jax
import jax.numpy as jnp
from jax import lax
from jax.experimental import pallas as pl
from jax.experimental.pallas import tpu as pltpu
from jax.sharding import PartitionSpec as P

SLOTS = 8
BF = jnp.bfloat16
F32 = jnp.float32


def gathered_rows(block, first, count, width):
    columns = []
    for step in range(count):
        rows = pl.ds(pl.multiple_of(first + step * width, width), width)
        columns.append(jnp.concatenate([block[m, rows, :] for m in range(SLOTS)], axis=0))
    return jnp.concatenate(columns, axis=1)


def masked_turned(slots, width, me, neighbors_ref, virt, virt_t):
    parts = [
        jnp.where(neighbors_ref[m, me] >= 0, virt[m * width : (m + 1) * width, :].astype(F32), 0.0)
        for m in range(SLOTS)
    ]
    turned = jnp.concatenate(parts, axis=0).T
    for at, k in enumerate(slots):
        live = neighbors_ref[k, me] >= 0
        virt_t[at * width : (at + 1) * width, :] = jnp.where(
            live, turned[at * width : (at + 1) * width, :], 0.0
        ).astype(BF)


def product_kernel(slots, width, chunks, neighbors_hbm, virt_hbm, block_hbm, *refs):
    outs = refs[-7 - len(slots) : -7]
    neighbors_ref, virt, virt_t, block, neighbors_sem, virt_sem, sems = refs[-7:]
    me = lax.axis_index("tensor")
    low, count = slots[0], len(slots)
    ri = block.shape[-1]
    size = block.shape[1] // chunks

    def block_copy(c):
        rows = pl.ds(pl.multiple_of(c * size, size), size)
        return pltpu.make_async_copy(block_hbm.at[0, :, rows, :], block.at[:, rows, :], sems.at[c])

    virt_copy = pltpu.make_async_copy(
        virt_hbm.at[0, :, pl.ds(low * width, count * width)], virt, virt_sem
    )
    neighbors_copy = pltpu.make_async_copy(neighbors_hbm, neighbors_ref, neighbors_sem)
    neighbors_copy.start()
    virt_copy.start()
    for c in range(chunks):
        block_copy(c).start()
    neighbors_copy.wait()
    virt_copy.wait()
    masked_turned(slots, width, me, neighbors_ref, virt, virt_t)

    @pl.loop(0, chunks)
    def _(c):
        block_copy(c).wait()
        for pair in range(size // width // 2):
            base = c * size + 2 * pair * width
            right = gathered_rows(block, base, 2, width)
            both = jnp.dot(virt_t[...], right, preferred_element_type=F32).astype(BF)
            for at in range(count):
                for half in range(2):
                    rows = pl.ds(pl.multiple_of(base + half * width, width), width)
                    outs[at][rows, :] = both[at * width : (at + 1) * width, half * ri : (half + 1) * ri]


def products(slots, neighbors, virt, blocks, chunks, after=None, near=False):
    pairs, ri = blocks.shape[2:]
    wide = virt.shape[1]
    width = wide // SLOTS
    count = len(slots)
    hbm = pl.BlockSpec(memory_space=pltpu.HBM)
    after = [] if after is None else [after]
    return pl.pallas_call(
        functools.partial(product_kernel, slots, width, chunks),
        in_specs=[hbm, hbm, hbm] + [pl.BlockSpec(memory_space=pl.ANY)] * len(after),
        out_specs=[pl.BlockSpec(memory_space=pltpu.VMEM)] * count,
        out_shape=[pltpu.VMEM((pairs, ri), BF) if near else pltpu.HBM((pairs, ri), BF)] * count,
        scratch_shapes=[
            pltpu.SMEM(neighbors.shape, jnp.int32),
            pltpu.VMEM((wide, count * width), BF),
            pltpu.VMEM((count * width, wide), BF),
            pltpu.VMEM((SLOTS, pairs, ri), BF),
            pltpu.SemaphoreType.DMA,
            pltpu.SemaphoreType.DMA,
            pltpu.SemaphoreType.DMA((chunks,)),
        ],
        compiler_params=pltpu.CompilerParams(vmem_limit_bytes=24 << 20),
        cost_estimate=pl.CostEstimate(flops=1, bytes_accessed=1, transcendentals=0),
        name="products",
    )(neighbors, virt, blocks, *after)


def turned_product_kernel(slots, width, chunks, slab, cuts, me_ref, neighbors_ref, virt_hbm, block_hbm, *refs):
    count = len(slots)
    outs = refs[-7 - sum(len(each) for each in cuts) : -7]
    virt, virt_t, block, sides, virt_sem, sems, out_sems = refs[-7:]
    me = me_ref[0]
    low = slots[0]
    ri = block.shape[-1]
    size = block.shape[1] // chunks

    def block_copy(c):
        rows = pl.ds(pl.multiple_of(c * size, size), size)
        return pltpu.make_async_copy(block_hbm.at[0, :, rows, :], block.at[:, rows, :], sems.at[c])

    virt_copy = pltpu.make_async_copy(
        virt_hbm.at[0, :, pl.ds(low * width, count * width)], virt, virt_sem
    )
    virt_copy.start()
    for c in range(chunks):
        block_copy(c).start()
    virt_copy.wait()
    masked_turned(slots, width, me, neighbors_ref, virt, virt_t)

    @pl.loop(0, chunks)
    def _(c):
        block_copy(c).wait()
        for pair in range(size // width // 2):
            base = c * size + 2 * pair * width
            right = gathered_rows(block, base, 2, width)
            both = jnp.dot(virt_t[...], right, preferred_element_type=F32).astype(BF)
            lanes = pl.ds(pl.multiple_of(base, 2 * width), 2 * width)
            for at in range(count):
                mine = both[at * width : (at + 1) * width, :]
                rows = jnp.concatenate([mine[:, :ri], mine[:, ri:]], axis=0)
                sides[at, :, lanes] = rows.T

    copies = []
    outs = list(outs)
    for at, k in enumerate(slots):
        chip = (me ^ k) >> 1
        for first, last in cuts[at]:
            out = outs.pop(0)
            for g in range(first, last):
                source = pl.ds(pl.multiple_of((chip ^ g) * slab, slab), slab)
                target = out.at[pl.ds((g - first) * slab, slab), :]
                copies.append(pltpu.make_async_copy(sides.at[at, source, :], target, out_sems.at[len(copies)]))
    for copy in copies:
        copy.start()
    for copy in copies:
        copy.wait()


def turned_products(slots, me, neighbors, virt, blocks, chunks, slab, cuts, after):
    pairs, ri = blocks.shape[2:]
    wide = virt.shape[1]
    width = wide // SLOTS
    count = len(slots)
    smem = pl.BlockSpec(memory_space=pltpu.SMEM)
    hbm = pl.BlockSpec(memory_space=pltpu.HBM)
    out = pl.pallas_call(
        functools.partial(turned_product_kernel, slots, width, chunks, slab, cuts),
        in_specs=[smem, smem, hbm, hbm, pl.BlockSpec(memory_space=pl.ANY)],
        out_specs=[hbm] * sum(len(each) for each in cuts),
        out_shape=[pltpu.HBM(((last - first) * slab, pairs), BF) for each in cuts for first, last in each],
        scratch_shapes=[
            pltpu.VMEM((wide, count * width), BF),
            pltpu.VMEM((count * width, wide), BF),
            pltpu.VMEM((SLOTS, pairs, ri), BF),
            pltpu.VMEM((count, ri, pairs), BF),
            pltpu.SemaphoreType.DMA,
            pltpu.SemaphoreType.DMA((chunks,)),
            pltpu.SemaphoreType.DMA((count * ri // slab,)),
        ],
        compiler_params=pltpu.CompilerParams(vmem_limit_bytes=24 << 20),
        cost_estimate=pl.CostEstimate(flops=1, bytes_accessed=1, transcendentals=0),
        name="turned_products",
    )(me, neighbors, virt, blocks, after)
    out = list(out)
    return {k: [out.pop(0) for _ in cuts[at]] for at, k in enumerate(slots)}


def project_kernel(width, rows, me_ref, neighbors_ref, occ_ref, block_ref, after_ref, *refs):
    outs, occ, turn = refs[:-2], refs[-2], refs[-1]
    me = me_ref[0]
    wide = SLOTS * width

    @pl.when(pl.program_id(0) == 0)
    def _():
        slot = lax.broadcasted_iota(jnp.int32, (1, wide), 1) // width
        keep = jnp.zeros((1, wide), F32)
        for n in range(SLOTS):
            keep = jnp.where((slot == n) & (neighbors_ref[n, me] >= 0), 1.0, keep)
        occ[...] = (occ_ref[0].astype(F32) * keep).astype(BF)

    ri = block_ref.shape[-1]
    for pair in range(rows // 2):
        right = gathered_rows(block_ref.at[0], 2 * pair * width, 2, width)
        both = jnp.dot(occ[...], right, preferred_element_type=F32)
        for half in range(2):
            turn[pl.ds(2 * pair + half, wide, stride=rows), :] = both[:, half * ri : (half + 1) * ri]
    for m in range(SLOTS):
        piece = turn[m * width * rows : (m + 1) * width * rows, :]
        outs[m][...] = piece.astype(BF).reshape(width, rows, ri)


def projections(me, neighbors, occ, blocks, after, rows=16):
    pairs, ri = blocks.shape[2:]
    wide = occ.shape[1]
    width = wide // SLOTS
    steps = width // rows
    chunk = rows * width
    smem = pl.BlockSpec(memory_space=pltpu.SMEM)
    out = pl.pallas_call(
        functools.partial(project_kernel, width, rows),
        grid=(steps,),
        in_specs=[
            smem,
            smem,
            pl.BlockSpec((1, wide, wide), lambda s: (0, 0, 0)),
            pl.BlockSpec((1, SLOTS, chunk, ri), lambda s: (0, 0, s, 0)),
            pl.BlockSpec(memory_space=pl.ANY),
        ],
        out_specs=[pl.BlockSpec((width, rows, ri), lambda s: (0, s, 0))] * SLOTS,
        out_shape=[(pltpu.VMEM if m in (2, 3, 4, 5) else pltpu.HBM)((width, width, ri), BF) for m in range(SLOTS)],
        scratch_shapes=[pltpu.VMEM((wide, wide), BF), pltpu.VMEM((wide * rows, ri), F32)],
        compiler_params=pltpu.CompilerParams(vmem_limit_bytes=17 << 20),
        cost_estimate=pl.CostEstimate(flops=1, bytes_accessed=1, transcendentals=0),
        name="projections",
    )(me, neighbors, occ, blocks, after)
    return [each.reshape(pairs, ri) for each in out]


def contract_kernel(count, has_start, *refs):
    out = refs[2 * count + has_start + (len(refs) - 2 * count - has_start - 1) // 2]
    total = refs[2 * count][...] if has_start else None
    for left, right in zip(refs[:count], refs[count : 2 * count]):
        term = lax.dot_general(left[...], right[...], (((0,), (0,)), ((), ())), preferred_element_type=F32)
        total = term if total is None else total + term
    out[...] = total


def contract(lefts, rights, start=None, passed=()):
    pairs, ri = rights[0].shape
    count = len(lefts)
    starts = [] if start is None else [start]
    vmem = pl.BlockSpec(memory_space=pltpu.VMEM)
    anywhere = pl.BlockSpec(memory_space=pl.ANY)
    return pl.pallas_call(
        functools.partial(contract_kernel, count, len(starts)),
        in_specs=[vmem] * (2 * count + len(starts)) + [anywhere] * len(passed),
        out_specs=[vmem] + [anywhere] * len(passed),
        out_shape=[pltpu.VMEM((ri, ri), F32)] + [pltpu.HBM(each.shape, each.dtype) for each in passed],
        input_output_aliases={2 * count + len(starts) + at: 1 + at for at in range(len(passed))},
        compiler_params=pltpu.CompilerParams(vmem_limit_bytes=8 << 20),
        cost_estimate=pl.CostEstimate(flops=1, bytes_accessed=1, transcendentals=0),
        name="contract",
    )(*lefts, *rights, *starts, *passed)


def rows_kernel(count, rows, slab, bases, after, me_ref, *refs):
    lefts, rights = refs[:count], refs[count : 2 * count]
    rest = refs[2 * count : 2 * count + len(bases)]
    skip = 2 * count + len(bases) + after
    skip += (len(refs) - skip - len(rows)) // 2
    outs = refs[skip : skip + len(rows)]
    chip = me_ref[0] >> 1
    height = sum(rows)
    total = jnp.zeros((height, rest[0].shape[1]), F32)
    for left, right in zip(lefts, rights):
        total += jnp.dot(left[...], right[...], preferred_element_type=F32)
    for base, (kind, first) in zip(rest, bases):
        if kind == "all":
            pieces = []
            for g in range(first, first + height // slab):
                pieces.append(base[pl.ds(pl.multiple_of((chip ^ g) * slab, slab), slab), :])
            total += jnp.concatenate(pieces, axis=0) if len(pieces) > 1 else pieces[0]
        else:
            total += base[first : first + height, :]
    at = 0
    for out, each in zip(outs, rows):
        out[...] = total[at : at + each, :]
        at += each


def contract_rows(me, lefts, rights, rows, slab, bases=(), passed=(), after=()):
    ri = bases[0][2].shape[1]
    count = len(lefts)
    vmem = pl.BlockSpec(memory_space=pltpu.VMEM)
    anywhere = pl.BlockSpec(memory_space=pl.ANY)
    kinds = tuple((kind, first) for kind, first, _ in bases)
    return pl.pallas_call(
        functools.partial(rows_kernel, count, rows, slab, kinds, len(after)),
        in_specs=[pl.BlockSpec(memory_space=pltpu.SMEM)]
        + [vmem] * (2 * count + len(bases) + len(after))
        + [anywhere] * len(passed),
        out_specs=[vmem] * len(rows) + [anywhere] * len(passed),
        out_shape=[pltpu.VMEM((each, ri), F32) for each in rows]
        + [pltpu.HBM(each.shape, each.dtype) for each in passed],
        input_output_aliases={1 + 2 * count + len(bases) + len(after) + at: len(rows) + at for at in range(len(passed))},
        compiler_params=pltpu.CompilerParams(vmem_limit_bytes=8 << 20),
        cost_estimate=pl.CostEstimate(flops=20_000_000_000, bytes_accessed=1, transcendentals=0),
        name="contract_rows",
    )(me, *lefts, *rights, *[array for _, _, array in bases], *after, *passed)


def exchange(value, k, devices):
    return lax.ppermute(value, "tensor", [(i, i ^ k) for i in range(devices)])


def reduce_rows(total, devices, order):
    index = lax.axis_index("tensor")
    bits = [1 << b for b in reversed(range(devices.bit_length() - 1))]
    value = total.reshape((2,) * len(bits) + (total.shape[0] // devices, total.shape[1]))
    left = list(bits)
    for k in order:
        at = left.index(k)
        left.pop(at)
        low = lax.index_in_dim(value, 0, at, keepdims=False)
        high = lax.index_in_dim(value, 1, at, keepdims=False)
        upper = (index & k) != 0
        value = jnp.where(upper, high, low) + exchange(jnp.where(upper, low, high), k, devices)
    return value


def local(devices, three_center, occ_green, virt_green, neighbors):
    me = lax.axis_index("tensor").astype(jnp.int32).reshape(1)
    by_slot = pltpu.with_memory_space_constraint(neighbors.T, pltpu.HBM)
    three_center = pltpu.with_memory_space_constraint(three_center, pltpu.HBM)
    occ_green = pltpu.with_memory_space_constraint(occ_green, pltpu.HBM)
    virt_green = pltpu.with_memory_space_constraint(virt_green, pltpu.HBM)
    sides = dict(zip((6, 7), products((6, 7), by_slot, virt_green, three_center, 2, near=True)))
    arrived = {k: exchange(sides[k], k, devices) for k in (6, 7)}
    middle = (2, 3, 4, 5)
    slab = 2 * three_center.shape[-1] // devices
    by_owner = devices == 16 and slab == 16
    if by_owner:
        cuts = (((3, 8), (0, 3)), ((3, 8), (1, 3), (0, 1))) * 2
        pieces = turned_products(
            middle, me, by_slot, virt_green, three_center, 4, slab, cuts, sides[6]
        )
        latest = pieces[5][0]
    else:
        sides.update(zip(middle, products(middle, by_slot, virt_green, three_center, 4, sides[6])))
        for k in middle:
            arrived[k] = exchange(sides[k], k, devices)
        latest = sides[5]
    sides.update(zip((0, 1), products((0, 1), by_slot, virt_green, three_center, 2, latest)))
    project = projections(me, by_slot, occ_green, three_center, sides[0])
    arrived[0] = sides[0]
    arrived[1] = exchange(sides[1], 1, devices)
    first, second = (4, 2), (5, 3)
    passed = [pieces[k][0] for k in second] if by_owner else []
    total, *passed = contract([arrived[k] for k in (6, 0)], [project[k] for k in (6, 0)], None, passed)
    if not by_owner:
        for group in ((7, 1), first, second):
            (total,) = contract([arrived[k] for k in group], [project[k] for k in group], total)
        bits = [1 << b for b in reversed(range(devices.bit_length() - 1))]
        return reduce_rows(total, devices, bits)

    def send(values, slots):
        return [exchange(value, k, devices) for k, value in zip(slots, values)]

    first_rights = [project[k] for k in first]
    second_rights = [project[k] for k in second]
    first_far = send([pieces[k][0] for k in first], first)
    second_far = send(passed, second)
    (total,) = contract([arrived[k] for k in (7, 1)], [project[k] for k in (7, 1)], total)
    outer, *passed = contract_rows(
        me, first_far, first_rights, (5 * slab,), slab, [("all", 3, total)], [pieces[k][1] for k in first]
    )
    first_own = send(passed, first)
    across, outer, *passed = contract_rows(
        me, second_far, second_rights, (slab, 4 * slab), slab, [("own", 0, outer)], [pieces[k][1] for k in second]
    )
    inner = exchange(outer, 8, devices)
    second_mid = send(passed, second)
    chip, rest, *passed = contract_rows(
        me, first_own, first_rights, (slab, 2 * slab), slab, [("all", 0, total)], [pieces[k][2] for k in second]
    )
    second_near = send(passed, second)
    across = exchange(across + inner[3 * slab :], 6, devices)
    square = contract_rows(
        me, second_mid, second_rights, (slab, slab), slab, [("own", 0, rest), ("own", slab, inner)]
    )
    square = [exchange(square[at], 2 * (at + 1), devices) for at in (1, 0)]
    (chip,) = contract_rows(
        me, second_near, second_rights, (slab,), slab, [("own", 0, chip), ("own", 0, inner)]
    )
    chip = chip + across + square[0] + square[1]
    half = slab // 2
    upper = (lax.axis_index("tensor") & 1) != 0
    keep = jnp.where(upper, chip[half:], chip[:half])
    return keep + exchange(jnp.where(upper, chip[:half], chip[half:]), 1, devices)


def solution(mesh):
    devices = mesh.shape["tensor"]
    in_specs = (
        P(("group", "tensor"), None, None, None),
        P("tensor", None, None),
        P("tensor", None, None),
        P(),
    )
    out_specs = P(("group", "tensor"), None)
    return jax.shard_map(
        functools.partial(local, devices), mesh=mesh, in_specs=in_specs, out_specs=out_specs, check_vma=False
    )
```

```python
import functools

import jax
import jax.numpy as jnp
from jax import lax
from jax.experimental import pallas as pl
from jax.experimental.pallas import tpu as pltpu
from jax.sharding import PartitionSpec as P

SLOTS = 8
BF = jnp.bfloat16
F32 = jnp.float32


def gathered_rows(block, first, count, width):
    columns = []
    for step in range(count):
        rows = pl.ds(pl.multiple_of(first + step * width, width), width)
        columns.append(jnp.concatenate([block[m, rows, :] for m in range(SLOTS)], axis=0))
    return jnp.concatenate(columns, axis=1)


def masked_turned(slots, width, me, neighbors_ref, virt, virt_t):
    for pair in range(len(slots) // 2):
        parts = [
            jnp.where(neighbors_ref[m, me] >= 0, virt[pair, m * width : (m + 1) * width, :].astype(F32), 0.0)
            for m in range(SLOTS)
        ]
        turned = jnp.concatenate(parts, axis=0).T
        for at in range(2):
            live = neighbors_ref[slots[2 * pair + at], me] >= 0
            virt_t[(2 * pair + at) * width : (2 * pair + at + 1) * width, :] = jnp.where(
                live, turned[at * width : (at + 1) * width, :], 0.0
            ).astype(BF)


def virt_copies(slots, width, virt_hbm, virt, sems):
    return [
        pltpu.make_async_copy(
            virt_hbm.at[0, :, pl.ds(k * width, 2 * width)], virt.at[pair], sems.at[pair]
        )
        for pair, k in enumerate(slots[::2])
    ]


def product_kernel(slots, wanted, width, chunks, neighbors_hbm, virt_hbm, block_hbm, *refs):
    outs = refs[-7 - len(wanted) : -7]
    neighbors_ref, virt, virt_t, block, neighbors_sem, virt_sems, sems = refs[-7:]
    me = lax.axis_index("tensor")
    ri = block.shape[-1]
    size = block_hbm.shape[2] // chunks
    start = min(first for _, first, _ in wanted)
    stop = max(last for _, _, last in wanted)

    def block_copy(c):
        rows = pl.ds(pl.multiple_of((c - start) * size, size), size)
        source = pl.ds(pl.multiple_of(c * size, size), size)
        return pltpu.make_async_copy(block_hbm.at[0, :, source, :], block.at[:, rows, :], sems.at[c - start])

    neighbors_copy = pltpu.make_async_copy(neighbors_hbm, neighbors_ref, neighbors_sem)
    neighbors_copy.start()
    copies = virt_copies(slots, width, virt_hbm, virt, virt_sems)
    for copy in copies:
        copy.start()
    for c in range(start, stop):
        block_copy(c).start()
    neighbors_copy.wait()
    for copy in copies:
        copy.wait()
    masked_turned(slots, width, me, neighbors_ref, virt, virt_t)

    def run(begin, end, busy):
        low = min(wanted[at][0] for at in busy) * width
        high = (max(wanted[at][0] for at in busy) + 1) * width

        @pl.loop(begin, end)
        def _(c):
            block_copy(c).wait()
            for pair in range(size // width // 2):
                inner = 2 * pair * width
                right = gathered_rows(block, (c - start) * size + inner, 2, width)
                both = jnp.dot(virt_t[low:high, :], right, preferred_element_type=F32).astype(BF)
                for at in busy:
                    row = wanted[at][0] * width - low
                    for half in range(2):
                        base = (c - wanted[at][1]) * size + inner + half * width
                        rows = pl.ds(pl.multiple_of(base, width), width)
                        outs[at][rows, :] = both[row : row + width, half * ri : (half + 1) * ri]

    edges = sorted({edge for _, *each in wanted for edge in each})
    for begin, end in zip(edges, edges[1:]):
        run(begin, end, [at for at, (_, first, last) in enumerate(wanted) if first <= begin and end <= last])


def products(slots, neighbors, virt, blocks, chunks, after=(), near=False, wanted=None):
    pairs, ri = blocks.shape[2:]
    wide = virt.shape[1]
    width = wide // SLOTS
    count = len(slots)
    wanted = wanted or tuple((at, 0, chunks) for at in range(count))
    used = max(last for _, _, last in wanted) - min(first for _, first, _ in wanted)
    shapes = [(pairs // chunks * (last - first), ri) for _, first, last in wanted]
    hbm = pl.BlockSpec(memory_space=pltpu.HBM)
    return pl.pallas_call(
        functools.partial(product_kernel, slots, wanted, width, chunks),
        in_specs=[hbm, hbm, hbm] + [pl.BlockSpec(memory_space=pl.ANY)] * len(after),
        out_specs=[pl.BlockSpec(memory_space=pltpu.VMEM)] * len(wanted),
        out_shape=[(pltpu.VMEM if near else pltpu.HBM)(shape, BF) for shape in shapes],
        scratch_shapes=[
            pltpu.SMEM(neighbors.shape, jnp.int32),
            pltpu.VMEM((count // 2, wide, 2 * width), BF),
            pltpu.VMEM((count * width, wide), BF),
            pltpu.VMEM((SLOTS, pairs // chunks * used, ri), BF),
            pltpu.SemaphoreType.DMA,
            pltpu.SemaphoreType.DMA((count // 2,)),
            pltpu.SemaphoreType.DMA((used,)),
        ],
        compiler_params=pltpu.CompilerParams(vmem_limit_bytes=24 << 20),
        cost_estimate=pl.CostEstimate(flops=1, bytes_accessed=1, transcendentals=0),
        name="products",
    )(neighbors, virt, blocks, *after)


def turned_product_kernel(slots, width, chunks, slab, cuts, neighbors_hbm, virt_hbm, block_hbm, *refs):
    count = len(slots)
    pieces = sum(len(each) for each in cuts)
    outs = refs[-9 - pieces : -9]
    neighbors_ref, virt, virt_t, block, sides, neighbors_sem, virt_sems, sems, out_sems = refs[-9:]
    me = lax.axis_index("tensor")
    ri = block.shape[-1]
    size = block.shape[1] // chunks

    def block_copy(c):
        rows = pl.ds(pl.multiple_of(c * size, size), size)
        return pltpu.make_async_copy(block_hbm.at[0, :, rows, :], block.at[:, rows, :], sems.at[c])

    neighbors_copy = pltpu.make_async_copy(neighbors_hbm, neighbors_ref, neighbors_sem)
    neighbors_copy.start()
    virt_moves = virt_copies(slots, width, virt_hbm, virt, virt_sems)
    for copy in virt_moves:
        copy.start()
    for c in range(chunks):
        block_copy(c).start()
    neighbors_copy.wait()
    for copy in virt_moves:
        copy.wait()
    masked_turned(slots, width, me, neighbors_ref, virt, virt_t)

    @pl.loop(0, chunks)
    def _(c):
        block_copy(c).wait()
        for pair in range(size // width // 2):
            base = c * size + 2 * pair * width
            right = gathered_rows(block, base, 2, width)
            both = jnp.dot(virt_t[...], right, preferred_element_type=F32).astype(BF)
            lanes = pl.ds(pl.multiple_of(base, 2 * width), 2 * width)
            for at in range(count):
                mine = both[at * width : (at + 1) * width, :]
                rows = jnp.concatenate([mine[:, :ri], mine[:, ri:]], axis=0)
                sides[at, :, lanes] = rows.T

    copies = []
    outs = list(outs)
    for at, k in enumerate(slots):
        chip = (me ^ k) >> 1
        for first, last in cuts[at]:
            out = outs.pop(0)
            for g in range(first, last):
                source = pl.ds(pl.multiple_of((chip ^ g) * slab, slab), slab)
                target = out.at[pl.ds((g - first) * slab, slab), :]
                copies.append(pltpu.make_async_copy(sides.at[at, source, :], target, out_sems.at[len(copies)]))
    for copy in copies:
        copy.start()
    for copy in copies:
        copy.wait()


def turned_products(slots, neighbors, virt, blocks, chunks, slab, cuts, after):
    pairs, ri = blocks.shape[2:]
    wide = virt.shape[1]
    width = wide // SLOTS
    count = len(slots)
    hbm = pl.BlockSpec(memory_space=pltpu.HBM)
    out = pl.pallas_call(
        functools.partial(turned_product_kernel, slots, width, chunks, slab, cuts),
        in_specs=[hbm, hbm, hbm, pl.BlockSpec(memory_space=pl.ANY)],
        out_specs=[hbm] * sum(len(each) for each in cuts),
        out_shape=[pltpu.HBM(((last - first) * slab, pairs), BF) for each in cuts for first, last in each],
        scratch_shapes=[
            pltpu.SMEM(neighbors.shape, jnp.int32),
            pltpu.VMEM((count // 2, wide, 2 * width), BF),
            pltpu.VMEM((count * width, wide), BF),
            pltpu.VMEM((SLOTS, pairs, ri), BF),
            pltpu.VMEM((count, ri, pairs), BF),
            pltpu.SemaphoreType.DMA,
            pltpu.SemaphoreType.DMA((count // 2,)),
            pltpu.SemaphoreType.DMA((chunks,)),
            pltpu.SemaphoreType.DMA((count * ri // slab,)),
        ],
        compiler_params=pltpu.CompilerParams(vmem_limit_bytes=24 << 20),
        cost_estimate=pl.CostEstimate(flops=1, bytes_accessed=1, transcendentals=0),
        name="turned_products",
    )(neighbors, virt, blocks, after)
    out = list(out)
    return {k: [out.pop(0) for _ in cuts[at]] for at, k in enumerate(slots)}


def project_kernel(width, rows, me_ref, neighbors_ref, occ_ref, block_ref, after_ref, *refs):
    outs, occ, turn = refs[:-2], refs[-2], refs[-1]
    me = me_ref[0]
    wide = SLOTS * width

    @pl.when(pl.program_id(0) == 0)
    def _():
        slot = lax.broadcasted_iota(jnp.int32, (1, wide), 1) // width
        keep = jnp.zeros((1, wide), F32)
        for n in range(SLOTS):
            keep = jnp.where((slot == n) & (neighbors_ref[n, me] >= 0), 1.0, keep)
        occ[...] = (occ_ref[0].astype(F32) * keep).astype(BF)

    ri = block_ref.shape[-1]
    for pair in range(rows // 2):
        right = gathered_rows(block_ref.at[0], 2 * pair * width, 2, width)
        both = jnp.dot(occ[...], right, preferred_element_type=F32)
        for half in range(2):
            turn[pl.ds(2 * pair + half, wide, stride=rows), :] = both[:, half * ri : (half + 1) * ri]
    for m in range(SLOTS):
        piece = turn[m * width * rows : (m + 1) * width * rows, :]
        outs[m][...] = piece.astype(BF).reshape(width, rows, ri)


def projections(me, neighbors, occ, blocks, after, rows=16):
    pairs, ri = blocks.shape[2:]
    wide = occ.shape[1]
    width = wide // SLOTS
    steps = width // rows
    chunk = rows * width
    smem = pl.BlockSpec(memory_space=pltpu.SMEM)
    out = pl.pallas_call(
        functools.partial(project_kernel, width, rows),
        grid=(steps,),
        in_specs=[
            smem,
            smem,
            pl.BlockSpec((1, wide, wide), lambda s: (0, 0, 0)),
            pl.BlockSpec((1, SLOTS, chunk, ri), lambda s: (0, 0, s, 0)),
            pl.BlockSpec(memory_space=pl.ANY),
        ],
        out_specs=[pl.BlockSpec((width, rows, ri), lambda s: (0, s, 0))] * SLOTS,
        out_shape=[(pltpu.VMEM if m in (2, 3, 4, 5) else pltpu.HBM)((width, width, ri), BF) for m in range(SLOTS)],
        scratch_shapes=[pltpu.VMEM((wide, wide), BF), pltpu.VMEM((wide * rows, ri), F32)],
        compiler_params=pltpu.CompilerParams(vmem_limit_bytes=17 << 20),
        cost_estimate=pl.CostEstimate(flops=1, bytes_accessed=1, transcendentals=0),
        name="projections",
    )(me, neighbors, occ, blocks, after)
    return [each.reshape(pairs, ri) for each in out]


def contract_kernel(count, begins, has_start, *refs):
    out = refs[2 * count + has_start + (len(refs) - 2 * count - has_start - 1) // 2]
    total = refs[2 * count][...] if has_start else None
    for at, (left, right) in enumerate(zip(refs[:count], refs[count : 2 * count])):
        rows = pl.ds(begins[at], left.shape[0])
        term = lax.dot_general(left[...], right[rows, :], (((0,), (0,)), ((), ())), preferred_element_type=F32)
        total = term if total is None else total + term
    out[...] = total


def contract(lefts, rights, begins, start=None, passed=()):
    ri = rights[0].shape[1]
    count = len(lefts)
    starts = [] if start is None else [start]
    vmem = pl.BlockSpec(memory_space=pltpu.VMEM)
    anywhere = pl.BlockSpec(memory_space=pl.ANY)
    return pl.pallas_call(
        functools.partial(contract_kernel, count, begins, len(starts)),
        in_specs=[vmem] * (2 * count + len(starts)) + [anywhere] * len(passed),
        out_specs=[vmem] + [anywhere] * len(passed),
        out_shape=[pltpu.VMEM((ri, ri), F32)] + [pltpu.HBM(each.shape, each.dtype) for each in passed],
        input_output_aliases={2 * count + len(starts) + at: 1 + at for at in range(len(passed))},
        compiler_params=pltpu.CompilerParams(vmem_limit_bytes=8 << 20),
        cost_estimate=pl.CostEstimate(flops=1, bytes_accessed=1, transcendentals=0),
        name="contract",
    )(*lefts, *rights, *starts, *passed)


def rows_kernel(count, rows, slab, bases, after, me_ref, *refs):
    lefts, rights = refs[:count], refs[count : 2 * count]
    rest = refs[2 * count : 2 * count + len(bases)]
    skip = 2 * count + len(bases) + after
    skip += (len(refs) - skip - len(rows)) // 2
    outs = refs[skip : skip + len(rows)]
    chip = me_ref[0] >> 1
    height = sum(rows)
    total = jnp.zeros((height, rest[0].shape[1]), F32)
    for left, right in zip(lefts, rights):
        total += jnp.dot(left[...], right[...], preferred_element_type=F32)
    for base, (kind, first) in zip(rest, bases):
        if kind == "all":
            pieces = []
            for g in range(first, first + height // slab):
                pieces.append(base[pl.ds(pl.multiple_of((chip ^ g) * slab, slab), slab), :])
            total += jnp.concatenate(pieces, axis=0) if len(pieces) > 1 else pieces[0]
        else:
            total += base[first : first + height, :]
    at = 0
    for out, each in zip(outs, rows):
        out[...] = total[at : at + each, :]
        at += each


def contract_rows(me, lefts, rights, rows, slab, bases=(), passed=(), after=()):
    ri = bases[0][2].shape[1]
    count = len(lefts)
    vmem = pl.BlockSpec(memory_space=pltpu.VMEM)
    anywhere = pl.BlockSpec(memory_space=pl.ANY)
    kinds = tuple((kind, first) for kind, first, _ in bases)
    return pl.pallas_call(
        functools.partial(rows_kernel, count, rows, slab, kinds, len(after)),
        in_specs=[pl.BlockSpec(memory_space=pltpu.SMEM)]
        + [vmem] * (2 * count + len(bases) + len(after))
        + [anywhere] * len(passed),
        out_specs=[vmem] * len(rows) + [anywhere] * len(passed),
        out_shape=[pltpu.VMEM((each, ri), F32) for each in rows]
        + [pltpu.HBM(each.shape, each.dtype) for each in passed],
        input_output_aliases={1 + 2 * count + len(bases) + len(after) + at: len(rows) + at for at in range(len(passed))},
        compiler_params=pltpu.CompilerParams(vmem_limit_bytes=8 << 20),
        cost_estimate=pl.CostEstimate(flops=20_000_000_000, bytes_accessed=1, transcendentals=0),
        name="contract_rows",
    )(me, *lefts, *rights, *[array for _, _, array in bases], *after, *passed)


def exchange(value, k, devices):
    return lax.ppermute(value, "tensor", [(i, i ^ k) for i in range(devices)])


def reduce_rows(total, devices, order):
    index = lax.axis_index("tensor")
    bits = [1 << b for b in reversed(range(devices.bit_length() - 1))]
    value = total.reshape((2,) * len(bits) + (total.shape[0] // devices, total.shape[1]))
    left = list(bits)
    for k in order:
        at = left.index(k)
        left.pop(at)
        low = lax.index_in_dim(value, 0, at, keepdims=False)
        high = lax.index_in_dim(value, 1, at, keepdims=False)
        upper = (index & k) != 0
        value = jnp.where(upper, high, low) + exchange(jnp.where(upper, low, high), k, devices)
    return value


def local(devices, three_center, occ_green, virt_green, neighbors):
    me = lax.axis_index("tensor").astype(jnp.int32).reshape(1)
    by_slot = pltpu.with_memory_space_constraint(neighbors.T, pltpu.HBM)
    three_center = pltpu.with_memory_space_constraint(three_center, pltpu.HBM)
    occ_green = pltpu.with_memory_space_constraint(occ_green, pltpu.HBM)
    virt_green = pltpu.with_memory_space_constraint(virt_green, pltpu.HBM)
    middle, last = (2, 3, 4, 5), (6, 7)
    pairs = three_center.shape[2]
    slab = 2 * three_center.shape[-1] // devices
    by_owner = devices == 16 and slab == 16
    cuts = (((3, 8), (0, 3)), ((3, 8), (1, 3), (0, 1))) * 2 if by_owner else (((0, devices // 2),),) * 4
    begun = products(last, by_slot, virt_green, three_center, 2, near=True, wanted=((0, 0, 1), (1, 0, 1)))
    begun_in = [exchange(value, k, devices) for k, value in zip(last, begun)]
    own, *both = products(
        (0, 1) + last,
        by_slot,
        virt_green,
        three_center,
        4,
        begun[:1],
        wanted=((0, 0, 4), (1, 0, 2), (1, 2, 4), (2, 2, 4), (3, 2, 4)),
    )
    other, ended = both[:2], both[2:]
    ended_in = [exchange(value, k, devices) for k, value in zip(last, ended)]
    other_in = [exchange(value, 1, devices) for value in other]
    if by_owner:
        pieces = turned_products(middle, by_slot, virt_green, three_center, 4, slab, cuts, own)
        latest = pieces[5][0]
    else:
        sides = products(middle, by_slot, virt_green, three_center, 4, [own])
        arrived = {k: exchange(value, k, devices) for k, value in zip(middle, sides)}
        latest = sides[0]
    project = projections(me, by_slot, occ_green, three_center, latest)
    first, second = (4, 2), (5, 3)
    total, *passed = contract(
        [begun_in[0], own],
        [project[6], project[0]],
        (0, 0),
        None,
        [pieces[k][0] for k in second] if by_owner else [],
    )
    (total,) = contract([begun_in[1]], [project[7]], (0,), total)
    (total,) = contract(other_in, [project[1]] * 2, (0, pairs // 2), total)
    (total,) = contract(ended_in, [project[k] for k in last], (pairs // 2,) * 2, total)
    if not by_owner:
        for group in (first, second):
            (total,) = contract([arrived[k] for k in group], [project[k] for k in group], (0, 0), total)
        bits = [1 << b for b in reversed(range(devices.bit_length() - 1))]
        return reduce_rows(total, devices, bits)

    def send(values, slots):
        return [exchange(value, k, devices) for k, value in zip(slots, values)]

    first_rights = [project[k] for k in first]
    second_rights = [project[k] for k in second]
    first_far = send([pieces[k][0] for k in first], first)
    second_far = send(passed, second)
    outer, *passed = contract_rows(
        me, first_far, first_rights, (5 * slab,), slab, [("all", 3, total)], [pieces[k][1] for k in first]
    )
    first_own = send(passed, first)
    across, outer, *passed = contract_rows(
        me, second_far, second_rights, (slab, 4 * slab), slab, [("own", 0, outer)], [pieces[k][1] for k in second]
    )
    inner = exchange(outer, 8, devices)
    second_mid = send(passed, second)
    chip, rest, *passed = contract_rows(
        me, first_own, first_rights, (slab, 2 * slab), slab, [("all", 0, total)], [pieces[k][2] for k in second]
    )
    second_near = send(passed, second)
    across = exchange(across + inner[3 * slab :], 6, devices)
    square = contract_rows(
        me, second_mid, second_rights, (slab, slab), slab, [("own", 0, rest), ("own", slab, inner)]
    )
    square = [exchange(square[at], 2 * (at + 1), devices) for at in (1, 0)]
    (chip,) = contract_rows(
        me, second_near, second_rights, (slab,), slab, [("own", 0, chip), ("own", 0, inner)]
    )
    chip = chip + across + square[0] + square[1]
    half = slab // 2
    upper = (lax.axis_index("tensor") & 1) != 0
    keep = jnp.where(upper, chip[half:], chip[:half])
    return keep + exchange(jnp.where(upper, chip[:half], chip[half:]), 1, devices)


def solution(mesh):
    devices = mesh.shape["tensor"]
    in_specs = (
        P(("group", "tensor"), None, None, None),
        P("tensor", None, None),
        P("tensor", None, None),
        P(),
    )
    out_specs = P(("group", "tensor"), None)
    return jax.shard_map(
        functools.partial(local, devices), mesh=mesh, in_specs=in_specs, out_specs=out_specs, check_vma=False
    )
```

```python
import functools

import jax
import jax.numpy as jnp
from jax import lax
from jax.experimental import pallas as pl
from jax.experimental.pallas import tpu as pltpu
from jax.sharding import PartitionSpec as P

SLOTS = 8
BF = jnp.bfloat16
F32 = jnp.float32


def gathered_rows(block, first, count, width):
    columns = []
    for step in range(count):
        rows = pl.ds(pl.multiple_of(first + step * width, width), width)
        columns.append(jnp.concatenate([block[m, rows, :] for m in range(SLOTS)], axis=0))
    return jnp.concatenate(columns, axis=1)


def masked_turned(slots, width, me, neighbors_ref, virt, virt_t):
    for pair in range(len(slots) // 2):
        parts = [
            jnp.where(neighbors_ref[m, me] >= 0, virt[pair, m * width : (m + 1) * width, :].astype(F32), 0.0)
            for m in range(SLOTS)
        ]
        turned = jnp.concatenate(parts, axis=0).T
        for at in range(2):
            live = neighbors_ref[slots[2 * pair + at], me] >= 0
            virt_t[(2 * pair + at) * width : (2 * pair + at + 1) * width, :] = jnp.where(
                live, turned[at * width : (at + 1) * width, :], 0.0
            ).astype(BF)


def virt_copies(slots, width, virt_hbm, virt, sems):
    return [
        pltpu.make_async_copy(
            virt_hbm.at[0, :, pl.ds(k * width, 2 * width)], virt.at[pair], sems.at[pair]
        )
        for pair, k in enumerate(slots[::2])
    ]


def product_kernel(slots, wanted, width, chunks, neighbors_hbm, virt_hbm, block_hbm, *refs):
    outs = refs[-7 - len(wanted) : -7]
    neighbors_ref, virt, virt_t, block, neighbors_sem, virt_sems, sems = refs[-7:]
    me = lax.axis_index("tensor")
    ri = block.shape[-1]
    size = block_hbm.shape[2] // chunks
    start = min(first for _, first, _ in wanted)
    stop = max(last for _, _, last in wanted)

    def block_copy(c):
        rows = pl.ds(pl.multiple_of((c - start) * size, size), size)
        source = pl.ds(pl.multiple_of(c * size, size), size)
        return pltpu.make_async_copy(block_hbm.at[0, :, source, :], block.at[:, rows, :], sems.at[c - start])

    neighbors_copy = pltpu.make_async_copy(neighbors_hbm, neighbors_ref, neighbors_sem)
    neighbors_copy.start()
    copies = virt_copies(slots, width, virt_hbm, virt, virt_sems)
    for copy in copies:
        copy.start()
    for c in range(start, stop):
        block_copy(c).start()
    neighbors_copy.wait()
    for copy in copies:
        copy.wait()
    masked_turned(slots, width, me, neighbors_ref, virt, virt_t)

    def run(begin, end, busy):
        low = min(wanted[at][0] for at in busy) * width
        high = (max(wanted[at][0] for at in busy) + 1) * width

        @pl.loop(begin, end)
        def _(c):
            block_copy(c).wait()
            for pair in range(size // width // 2):
                inner = 2 * pair * width
                right = gathered_rows(block, (c - start) * size + inner, 2, width)
                both = jnp.dot(virt_t[low:high, :], right, preferred_element_type=F32).astype(BF)
                for at in busy:
                    row = wanted[at][0] * width - low
                    for half in range(2):
                        base = (c - wanted[at][1]) * size + inner + half * width
                        rows = pl.ds(pl.multiple_of(base, width), width)
                        outs[at][rows, :] = both[row : row + width, half * ri : (half + 1) * ri]

    edges = sorted({edge for _, *each in wanted for edge in each})
    for begin, end in zip(edges, edges[1:]):
        run(begin, end, [at for at, (_, first, last) in enumerate(wanted) if first <= begin and end <= last])


def products(slots, neighbors, virt, blocks, chunks, after=(), near=False, wanted=None):
    pairs, ri = blocks.shape[2:]
    wide = virt.shape[1]
    width = wide // SLOTS
    count = len(slots)
    wanted = wanted or tuple((at, 0, chunks) for at in range(count))
    used = max(last for _, _, last in wanted) - min(first for _, first, _ in wanted)
    shapes = [(pairs // chunks * (last - first), ri) for _, first, last in wanted]
    hbm = pl.BlockSpec(memory_space=pltpu.HBM)
    return pl.pallas_call(
        functools.partial(product_kernel, slots, wanted, width, chunks),
        in_specs=[hbm, hbm, hbm] + [pl.BlockSpec(memory_space=pl.ANY)] * len(after),
        out_specs=[pl.BlockSpec(memory_space=pltpu.VMEM)] * len(wanted),
        out_shape=[(pltpu.VMEM if near else pltpu.HBM)(shape, BF) for shape in shapes],
        scratch_shapes=[
            pltpu.SMEM(neighbors.shape, jnp.int32),
            pltpu.VMEM((count // 2, wide, 2 * width), BF),
            pltpu.VMEM((count * width, wide), BF),
            pltpu.VMEM((SLOTS, pairs // chunks * used, ri), BF),
            pltpu.SemaphoreType.DMA,
            pltpu.SemaphoreType.DMA((count // 2,)),
            pltpu.SemaphoreType.DMA((used,)),
        ],
        compiler_params=pltpu.CompilerParams(vmem_limit_bytes=24 << 20),
        cost_estimate=pl.CostEstimate(flops=1, bytes_accessed=1, transcendentals=0),
        name="products",
    )(neighbors, virt, blocks, *after)


def turned_product_kernel(slots, width, chunks, slab, cuts, neighbors_hbm, virt_hbm, block_hbm, *refs):
    count = len(slots)
    pieces = sum(len(each) for each in cuts)
    outs = refs[-9 - pieces : -9]
    neighbors_ref, virt, virt_t, block, sides, neighbors_sem, virt_sems, sems, out_sems = refs[-9:]
    me = lax.axis_index("tensor")
    ri = block.shape[-1]
    size = block.shape[1] // chunks

    def block_copy(c):
        rows = pl.ds(pl.multiple_of(c * size, size), size)
        return pltpu.make_async_copy(block_hbm.at[0, :, rows, :], block.at[:, rows, :], sems.at[c])

    neighbors_copy = pltpu.make_async_copy(neighbors_hbm, neighbors_ref, neighbors_sem)
    neighbors_copy.start()
    virt_moves = virt_copies(slots, width, virt_hbm, virt, virt_sems)
    for copy in virt_moves:
        copy.start()
    for c in range(chunks):
        block_copy(c).start()
    neighbors_copy.wait()
    for copy in virt_moves:
        copy.wait()
    masked_turned(slots, width, me, neighbors_ref, virt, virt_t)

    @pl.loop(0, chunks)
    def _(c):
        block_copy(c).wait()
        for pair in range(size // width // 2):
            base = c * size + 2 * pair * width
            right = gathered_rows(block, base, 2, width)
            both = jnp.dot(virt_t[...], right, preferred_element_type=F32).astype(BF)
            lanes = pl.ds(pl.multiple_of(base, 2 * width), 2 * width)
            for at in range(count):
                mine = both[at * width : (at + 1) * width, :]
                rows = jnp.concatenate([mine[:, :ri], mine[:, ri:]], axis=0)
                sides[at, :, lanes] = rows.T

    copies = []
    outs = list(outs)
    for at, k in enumerate(slots):
        chip = (me ^ k) >> 1
        for first, last in cuts[at]:
            out = outs.pop(0)
            for g in range(first, last):
                source = pl.ds(pl.multiple_of((chip ^ g) * slab, slab), slab)
                target = out.at[pl.ds((g - first) * slab, slab), :]
                copies.append(pltpu.make_async_copy(sides.at[at, source, :], target, out_sems.at[len(copies)]))
    for copy in copies:
        copy.start()
    for copy in copies:
        copy.wait()


def turned_products(slots, neighbors, virt, blocks, chunks, slab, cuts, after):
    pairs, ri = blocks.shape[2:]
    wide = virt.shape[1]
    width = wide // SLOTS
    count = len(slots)
    hbm = pl.BlockSpec(memory_space=pltpu.HBM)
    out = pl.pallas_call(
        functools.partial(turned_product_kernel, slots, width, chunks, slab, cuts),
        in_specs=[hbm, hbm, hbm, pl.BlockSpec(memory_space=pl.ANY)],
        out_specs=[hbm] * sum(len(each) for each in cuts),
        out_shape=[pltpu.HBM(((last - first) * slab, pairs), BF) for each in cuts for first, last in each],
        scratch_shapes=[
            pltpu.SMEM(neighbors.shape, jnp.int32),
            pltpu.VMEM((count // 2, wide, 2 * width), BF),
            pltpu.VMEM((count * width, wide), BF),
            pltpu.VMEM((SLOTS, pairs, ri), BF),
            pltpu.VMEM((count, ri, pairs), BF),
            pltpu.SemaphoreType.DMA,
            pltpu.SemaphoreType.DMA((count // 2,)),
            pltpu.SemaphoreType.DMA((chunks,)),
            pltpu.SemaphoreType.DMA((count * ri // slab,)),
        ],
        compiler_params=pltpu.CompilerParams(vmem_limit_bytes=24 << 20),
        cost_estimate=pl.CostEstimate(flops=1, bytes_accessed=1, transcendentals=0),
        name="turned_products",
    )(neighbors, virt, blocks, after)
    out = list(out)
    return {k: [out.pop(0) for _ in cuts[at]] for at, k in enumerate(slots)}


def project_kernel(width, rows, me_ref, neighbors_ref, occ_ref, block_ref, after_ref, *refs):
    outs, occ, turn = refs[:-2], refs[-2], refs[-1]
    me = me_ref[0]
    wide = SLOTS * width

    @pl.when(pl.program_id(0) == 0)
    def _():
        slot = lax.broadcasted_iota(jnp.int32, (1, wide), 1) // width
        keep = jnp.zeros((1, wide), F32)
        for n in range(SLOTS):
            keep = jnp.where((slot == n) & (neighbors_ref[n, me] >= 0), 1.0, keep)
        occ[...] = (occ_ref[0].astype(F32) * keep).astype(BF)

    ri = block_ref.shape[-1]
    for pair in range(rows // 2):
        right = gathered_rows(block_ref.at[0], 2 * pair * width, 2, width)
        both = jnp.dot(occ[...], right, preferred_element_type=F32)
        for half in range(2):
            turn[pl.ds(2 * pair + half, wide, stride=rows), :] = both[:, half * ri : (half + 1) * ri]
    for m in range(SLOTS):
        piece = turn[m * width * rows : (m + 1) * width * rows, :]
        outs[m][...] = piece.astype(BF).reshape(width, rows, ri)


def projections(me, neighbors, occ, blocks, after, rows=16):
    pairs, ri = blocks.shape[2:]
    wide = occ.shape[1]
    width = wide // SLOTS
    steps = width // rows
    chunk = rows * width
    smem = pl.BlockSpec(memory_space=pltpu.SMEM)
    out = pl.pallas_call(
        functools.partial(project_kernel, width, rows),
        grid=(steps,),
        in_specs=[
            smem,
            smem,
            pl.BlockSpec((1, wide, wide), lambda s: (0, 0, 0)),
            pl.BlockSpec((1, SLOTS, chunk, ri), lambda s: (0, 0, s, 0)),
            pl.BlockSpec(memory_space=pl.ANY),
        ],
        out_specs=[pl.BlockSpec((width, rows, ri), lambda s: (0, s, 0))] * SLOTS,
        out_shape=[(pltpu.VMEM if m in (2, 3, 4, 5) else pltpu.HBM)((width, width, ri), BF) for m in range(SLOTS)],
        scratch_shapes=[pltpu.VMEM((wide, wide), BF), pltpu.VMEM((wide * rows, ri), F32)],
        compiler_params=pltpu.CompilerParams(vmem_limit_bytes=17 << 20),
        cost_estimate=pl.CostEstimate(flops=1, bytes_accessed=1, transcendentals=0),
        name="projections",
    )(me, neighbors, occ, blocks, after)
    return [each.reshape(pairs, ri) for each in out]


def contract_kernel(count, begins, has_start, *refs):
    out = refs[2 * count + has_start + (len(refs) - 2 * count - has_start - 1) // 2]
    total = refs[2 * count][...] if has_start else None
    for at, (left, right) in enumerate(zip(refs[:count], refs[count : 2 * count])):
        rows = pl.ds(begins[at], left.shape[0])
        term = lax.dot_general(left[...], right[rows, :], (((0,), (0,)), ((), ())), preferred_element_type=F32)
        total = term if total is None else total + term
    out[...] = total


def contract(lefts, rights, begins, start=None, passed=()):
    ri = rights[0].shape[1]
    count = len(lefts)
    starts = [] if start is None else [start]
    vmem = pl.BlockSpec(memory_space=pltpu.VMEM)
    anywhere = pl.BlockSpec(memory_space=pl.ANY)
    return pl.pallas_call(
        functools.partial(contract_kernel, count, begins, len(starts)),
        in_specs=[vmem] * (2 * count + len(starts)) + [anywhere] * len(passed),
        out_specs=[vmem] + [anywhere] * len(passed),
        out_shape=[pltpu.VMEM((ri, ri), F32)] + [pltpu.HBM(each.shape, each.dtype) for each in passed],
        input_output_aliases={2 * count + len(starts) + at: 1 + at for at in range(len(passed))},
        compiler_params=pltpu.CompilerParams(vmem_limit_bytes=8 << 20),
        cost_estimate=pl.CostEstimate(flops=1, bytes_accessed=1, transcendentals=0),
        name="contract",
    )(*lefts, *rights, *starts, *passed)


def rows_kernel(count, rows, slab, bases, after, me_ref, *refs):
    lefts, rights = refs[:count], refs[count : 2 * count]
    rest = refs[2 * count : 2 * count + len(bases)]
    skip = 2 * count + len(bases) + after
    skip += (len(refs) - skip - len(rows)) // 2
    outs = refs[skip : skip + len(rows)]
    chip = me_ref[0] >> 1
    height = sum(rows)
    total = jnp.zeros((height, rest[0].shape[1]), F32)
    for left, right in zip(lefts, rights):
        total += jnp.dot(left[...], right[...], preferred_element_type=F32)
    for base, (kind, first) in zip(rest, bases):
        if kind == "all":
            pieces = []
            for g in range(first, first + height // slab):
                pieces.append(base[pl.ds(pl.multiple_of((chip ^ g) * slab, slab), slab), :])
            total += jnp.concatenate(pieces, axis=0) if len(pieces) > 1 else pieces[0]
        else:
            total += base[first : first + height, :]
    at = 0
    for out, each in zip(outs, rows):
        out[...] = total[at : at + each, :]
        at += each


def contract_rows(me, lefts, rights, rows, slab, bases=(), passed=(), after=()):
    ri = bases[0][2].shape[1]
    count = len(lefts)
    vmem = pl.BlockSpec(memory_space=pltpu.VMEM)
    anywhere = pl.BlockSpec(memory_space=pl.ANY)
    kinds = tuple((kind, first) for kind, first, _ in bases)
    return pl.pallas_call(
        functools.partial(rows_kernel, count, rows, slab, kinds, len(after)),
        in_specs=[pl.BlockSpec(memory_space=pltpu.SMEM)]
        + [vmem] * (2 * count + len(bases) + len(after))
        + [anywhere] * len(passed),
        out_specs=[vmem] * len(rows) + [anywhere] * len(passed),
        out_shape=[pltpu.VMEM((each, ri), F32) for each in rows]
        + [pltpu.HBM(each.shape, each.dtype) for each in passed],
        input_output_aliases={1 + 2 * count + len(bases) + len(after) + at: len(rows) + at for at in range(len(passed))},
        compiler_params=pltpu.CompilerParams(vmem_limit_bytes=8 << 20),
        cost_estimate=pl.CostEstimate(flops=20_000_000_000, bytes_accessed=1, transcendentals=0),
        name="contract_rows",
    )(me, *lefts, *rights, *[array for _, _, array in bases], *after, *passed)


def exchange(value, k, devices):
    return lax.ppermute(value, "tensor", [(i, i ^ k) for i in range(devices)])


def reduce_rows(total, devices, order):
    index = lax.axis_index("tensor")
    bits = [1 << b for b in reversed(range(devices.bit_length() - 1))]
    value = total.reshape((2,) * len(bits) + (total.shape[0] // devices, total.shape[1]))
    left = list(bits)
    for k in order:
        at = left.index(k)
        left.pop(at)
        low = lax.index_in_dim(value, 0, at, keepdims=False)
        high = lax.index_in_dim(value, 1, at, keepdims=False)
        upper = (index & k) != 0
        value = jnp.where(upper, high, low) + exchange(jnp.where(upper, low, high), k, devices)
    return value


def local(devices, three_center, occ_green, virt_green, neighbors):
    me = lax.axis_index("tensor").astype(jnp.int32).reshape(1)
    by_slot = pltpu.with_memory_space_constraint(neighbors.T, pltpu.HBM)
    three_center = pltpu.with_memory_space_constraint(three_center, pltpu.HBM)
    occ_green = pltpu.with_memory_space_constraint(occ_green, pltpu.HBM)
    virt_green = pltpu.with_memory_space_constraint(virt_green, pltpu.HBM)
    middle, last = (2, 3, 4, 5), (6, 7)
    pairs = three_center.shape[2]
    slab = 2 * three_center.shape[-1] // devices
    by_owner = devices == 16 and slab == 16
    cuts = (((3, 8), (0, 3)), ((3, 8), (1, 3), (0, 1))) * 2 if by_owner else (((0, devices // 2),),) * 4
    begun = products(last, by_slot, virt_green, three_center, 8, near=True, wanted=((0, 0, 2), (1, 0, 2)))
    begun_in = [exchange(value, k, devices) for k, value in zip(last, begun)]
    own, *both = products(
        (0, 1) + last,
        by_slot,
        virt_green,
        three_center,
        4,
        begun[:1],
        wanted=((0, 0, 4), (1, 0, 1), (1, 1, 2), (1, 2, 3), (1, 3, 4), (2, 1, 4), (3, 1, 4)),
    )
    other, ended = both[:4], both[4:]
    ended_in = [exchange(value, k, devices) for k, value in zip(last, ended)]
    other_in = [exchange(value, 1, devices) for value in other]
    if by_owner:
        pieces = turned_products(middle, by_slot, virt_green, three_center, 4, slab, cuts, own)
        latest = pieces[5][0]
    else:
        sides = products(middle, by_slot, virt_green, three_center, 4, [own])
        arrived = {k: exchange(value, k, devices) for k, value in zip(middle, sides)}
        latest = sides[0]
    project = projections(me, by_slot, occ_green, three_center, latest)
    first, second = (4, 2), (5, 3)
    total, *passed = contract(
        [begun_in[0], own],
        [project[6], project[0]],
        (0, 0),
        None,
        [pieces[k][0] for k in second] if by_owner else [],
    )
    (total,) = contract([begun_in[1]], [project[7]], (0,), total)
    (total,) = contract(other_in, [project[1]] * 4, [at * pairs // 4 for at in range(4)], total)
    (total,) = contract(ended_in, [project[k] for k in last], (pairs // 4,) * 2, total)
    if not by_owner:
        for group in (first, second):
            (total,) = contract([arrived[k] for k in group], [project[k] for k in group], (0, 0), total)
        bits = [1 << b for b in reversed(range(devices.bit_length() - 1))]
        return reduce_rows(total, devices, bits)

    def send(values, slots):
        return [exchange(value, k, devices) for k, value in zip(slots, values)]

    first_rights = [project[k] for k in first]
    second_rights = [project[k] for k in second]
    first_far = send([pieces[k][0] for k in first], first)
    second_far = send(passed, second)
    outer, *passed = contract_rows(
        me, first_far, first_rights, (5 * slab,), slab, [("all", 3, total)], [pieces[k][1] for k in first]
    )
    first_own = send(passed, first)
    across, outer, *passed = contract_rows(
        me, second_far, second_rights, (slab, 4 * slab), slab, [("own", 0, outer)], [pieces[k][1] for k in second]
    )
    inner = exchange(outer, 8, devices)
    second_mid = send(passed, second)
    chip, rest, *passed = contract_rows(
        me, first_own, first_rights, (slab, 2 * slab), slab, [("all", 0, total)], [pieces[k][2] for k in second]
    )
    second_near = send(passed, second)
    across = exchange(across + inner[3 * slab :], 6, devices)
    square = contract_rows(
        me, second_mid, second_rights, (slab, slab), slab, [("own", 0, rest), ("own", slab, inner)]
    )
    square = [exchange(square[at], 2 * (at + 1), devices) for at in (1, 0)]
    (chip,) = contract_rows(
        me, second_near, second_rights, (slab,), slab, [("own", 0, chip), ("own", 0, inner)]
    )
    chip = chip + across + square[0] + square[1]
    half = slab // 2
    upper = (lax.axis_index("tensor") & 1) != 0
    keep = jnp.where(upper, chip[half:], chip[:half])
    return keep + exchange(jnp.where(upper, chip[:half], chip[half:]), 1, devices)


def solution(mesh):
    devices = mesh.shape["tensor"]
    in_specs = (
        P(("group", "tensor"), None, None, None),
        P("tensor", None, None),
        P("tensor", None, None),
        P(),
    )
    out_specs = P(("group", "tensor"), None)
    return jax.shard_map(
        functools.partial(local, devices), mesh=mesh, in_specs=in_specs, out_specs=out_specs, check_vma=False
    )
```

```python
import functools

import jax
import jax.numpy as jnp
from jax import lax
from jax.experimental import pallas as pl
from jax.experimental.pallas import tpu as pltpu
from jax.sharding import PartitionSpec as P

SLOTS = 8
BF = jnp.bfloat16
F32 = jnp.float32


def gathered_rows(block, first, count, width):
    columns = []
    for step in range(count):
        rows = pl.ds(pl.multiple_of(first + step * width, width), width)
        columns.append(jnp.concatenate([block[m, rows, :] for m in range(SLOTS)], axis=0))
    return jnp.concatenate(columns, axis=1)


def masked_turned(slots, width, me, neighbors_ref, virt, virt_t):
    for pair in range(len(slots) // 2):
        parts = [
            jnp.where(neighbors_ref[m, me] >= 0, virt[pair, m * width : (m + 1) * width, :].astype(F32), 0.0)
            for m in range(SLOTS)
        ]
        turned = jnp.concatenate(parts, axis=0).T
        for at in range(2):
            live = neighbors_ref[slots[2 * pair + at], me] >= 0
            virt_t[(2 * pair + at) * width : (2 * pair + at + 1) * width, :] = jnp.where(
                live, turned[at * width : (at + 1) * width, :], 0.0
            ).astype(BF)


def virt_copies(slots, width, virt_hbm, virt, sems):
    return [
        pltpu.make_async_copy(
            virt_hbm.at[0, :, pl.ds(k * width, 2 * width)], virt.at[pair], sems.at[pair]
        )
        for pair, k in enumerate(slots[::2])
    ]


def product_kernel(slots, wanted, width, chunks, neighbors_hbm, virt_hbm, block_hbm, *refs):
    outs = refs[-7 - len(wanted) : -7]
    neighbors_ref, virt, virt_t, block, neighbors_sem, virt_sems, sems = refs[-7:]
    me = lax.axis_index("tensor")
    ri = block.shape[-1]
    size = block_hbm.shape[2] // chunks
    start = min(first for _, first, _ in wanted)
    stop = max(last for _, _, last in wanted)

    def block_copy(c):
        rows = pl.ds(pl.multiple_of((c - start) * size, size), size)
        source = pl.ds(pl.multiple_of(c * size, size), size)
        return pltpu.make_async_copy(block_hbm.at[0, :, source, :], block.at[:, rows, :], sems.at[c - start])

    neighbors_copy = pltpu.make_async_copy(neighbors_hbm, neighbors_ref, neighbors_sem)
    neighbors_copy.start()
    copies = virt_copies(slots, width, virt_hbm, virt, virt_sems)
    for copy in copies:
        copy.start()
    for c in range(start, stop):
        block_copy(c).start()
    neighbors_copy.wait()
    for copy in copies:
        copy.wait()
    masked_turned(slots, width, me, neighbors_ref, virt, virt_t)

    def run(begin, end, busy):
        low = min(wanted[at][0] for at in busy) * width
        high = (max(wanted[at][0] for at in busy) + 1) * width

        @pl.loop(begin, end)
        def _(c):
            block_copy(c).wait()
            for pair in range(size // width // 2):
                inner = 2 * pair * width
                right = gathered_rows(block, (c - start) * size + inner, 2, width)
                both = jnp.dot(virt_t[low:high, :], right, preferred_element_type=F32).astype(BF)
                for at in busy:
                    row = wanted[at][0] * width - low
                    for half in range(2):
                        base = (c - wanted[at][1]) * size + inner + half * width
                        rows = pl.ds(pl.multiple_of(base, width), width)
                        outs[at][rows, :] = both[row : row + width, half * ri : (half + 1) * ri]

    edges = sorted({edge for _, *each in wanted for edge in each})
    for begin, end in zip(edges, edges[1:]):
        run(begin, end, [at for at, (_, first, last) in enumerate(wanted) if first <= begin and end <= last])


def products(slots, neighbors, virt, blocks, chunks, after=(), near=False, wanted=None):
    pairs, ri = blocks.shape[2:]
    wide = virt.shape[1]
    width = wide // SLOTS
    count = len(slots)
    wanted = wanted or tuple((at, 0, chunks) for at in range(count))
    used = max(last for _, _, last in wanted) - min(first for _, first, _ in wanted)
    shapes = [(pairs // chunks * (last - first), ri) for _, first, last in wanted]
    hbm = pl.BlockSpec(memory_space=pltpu.HBM)
    return pl.pallas_call(
        functools.partial(product_kernel, slots, wanted, width, chunks),
        in_specs=[hbm, hbm, hbm] + [pl.BlockSpec(memory_space=pl.ANY)] * len(after),
        out_specs=[pl.BlockSpec(memory_space=pltpu.VMEM)] * len(wanted),
        out_shape=[(pltpu.VMEM if near else pltpu.HBM)(shape, BF) for shape in shapes],
        scratch_shapes=[
            pltpu.SMEM(neighbors.shape, jnp.int32),
            pltpu.VMEM((count // 2, wide, 2 * width), BF),
            pltpu.VMEM((count * width, wide), BF),
            pltpu.VMEM((SLOTS, pairs // chunks * used, ri), BF),
            pltpu.SemaphoreType.DMA,
            pltpu.SemaphoreType.DMA((count // 2,)),
            pltpu.SemaphoreType.DMA((used,)),
        ],
        compiler_params=pltpu.CompilerParams(vmem_limit_bytes=24 << 20),
        cost_estimate=pl.CostEstimate(flops=1, bytes_accessed=1, transcendentals=0),
        name="products",
    )(neighbors, virt, blocks, *after)


def turned_product_kernel(slots, width, chunks, slab, cuts, neighbors_hbm, virt_hbm, block_hbm, *refs):
    count = len(slots)
    pieces = sum(len(each) for each in cuts)
    outs = refs[-9 - pieces : -9]
    neighbors_ref, virt, virt_t, block, sides, neighbors_sem, virt_sems, sems, out_sems = refs[-9:]
    me = lax.axis_index("tensor")
    ri = block.shape[-1]
    size = block.shape[1] // chunks

    def block_copy(c):
        rows = pl.ds(pl.multiple_of(c * size, size), size)
        return pltpu.make_async_copy(block_hbm.at[0, :, rows, :], block.at[:, rows, :], sems.at[c])

    neighbors_copy = pltpu.make_async_copy(neighbors_hbm, neighbors_ref, neighbors_sem)
    neighbors_copy.start()
    virt_moves = virt_copies(slots, width, virt_hbm, virt, virt_sems)
    for copy in virt_moves:
        copy.start()
    for c in range(chunks):
        block_copy(c).start()
    neighbors_copy.wait()
    for copy in virt_moves:
        copy.wait()
    masked_turned(slots, width, me, neighbors_ref, virt, virt_t)

    @pl.loop(0, chunks)
    def _(c):
        block_copy(c).wait()
        for pair in range(size // width // 2):
            base = c * size + 2 * pair * width
            right = gathered_rows(block, base, 2, width)
            both = jnp.dot(virt_t[...], right, preferred_element_type=F32).astype(BF)
            lanes = pl.ds(pl.multiple_of(base, 2 * width), 2 * width)
            for at in range(count):
                mine = both[at * width : (at + 1) * width, :]
                rows = jnp.concatenate([mine[:, :ri], mine[:, ri:]], axis=0)
                sides[at, :, lanes] = rows.T

    copies = []
    outs = list(outs)
    for at, k in enumerate(slots):
        chip = (me ^ k) >> 1
        for first, last in cuts[at]:
            out = outs.pop(0)
            for g in range(first, last):
                source = pl.ds(pl.multiple_of((chip ^ g) * slab, slab), slab)
                target = out.at[pl.ds((g - first) * slab, slab), :]
                copies.append(pltpu.make_async_copy(sides.at[at, source, :], target, out_sems.at[len(copies)]))
    for copy in copies:
        copy.start()
    for copy in copies:
        copy.wait()


def turned_products(slots, neighbors, virt, blocks, chunks, slab, cuts, after):
    pairs, ri = blocks.shape[2:]
    wide = virt.shape[1]
    width = wide // SLOTS
    count = len(slots)
    hbm = pl.BlockSpec(memory_space=pltpu.HBM)
    out = pl.pallas_call(
        functools.partial(turned_product_kernel, slots, width, chunks, slab, cuts),
        in_specs=[hbm, hbm, hbm, pl.BlockSpec(memory_space=pl.ANY)],
        out_specs=[hbm] * sum(len(each) for each in cuts),
        out_shape=[pltpu.HBM(((last - first) * slab, pairs), BF) for each in cuts for first, last in each],
        scratch_shapes=[
            pltpu.SMEM(neighbors.shape, jnp.int32),
            pltpu.VMEM((count // 2, wide, 2 * width), BF),
            pltpu.VMEM((count * width, wide), BF),
            pltpu.VMEM((SLOTS, pairs, ri), BF),
            pltpu.VMEM((count, ri, pairs), BF),
            pltpu.SemaphoreType.DMA,
            pltpu.SemaphoreType.DMA((count // 2,)),
            pltpu.SemaphoreType.DMA((chunks,)),
            pltpu.SemaphoreType.DMA((count * ri // slab,)),
        ],
        compiler_params=pltpu.CompilerParams(vmem_limit_bytes=24 << 20),
        cost_estimate=pl.CostEstimate(flops=1, bytes_accessed=1, transcendentals=0),
        name="turned_products",
    )(neighbors, virt, blocks, after)
    out = list(out)
    return {k: [out.pop(0) for _ in cuts[at]] for at, k in enumerate(slots)}


def project_kernel(width, rows, me_ref, neighbors_ref, occ_ref, block_ref, after_ref, *refs):
    outs, occ, turn = refs[:-2], refs[-2], refs[-1]
    me = me_ref[0]
    wide = SLOTS * width

    @pl.when(pl.program_id(0) == 0)
    def _():
        slot = lax.broadcasted_iota(jnp.int32, (1, wide), 1) // width
        keep = jnp.zeros((1, wide), F32)
        for n in range(SLOTS):
            keep = jnp.where((slot == n) & (neighbors_ref[n, me] >= 0), 1.0, keep)
        occ[...] = (occ_ref[0].astype(F32) * keep).astype(BF)

    ri = block_ref.shape[-1]
    for pair in range(rows // 2):
        right = gathered_rows(block_ref.at[0], 2 * pair * width, 2, width)
        both = jnp.dot(occ[...], right, preferred_element_type=F32)
        for half in range(2):
            turn[pl.ds(2 * pair + half, wide, stride=rows), :] = both[:, half * ri : (half + 1) * ri]
    for m in range(SLOTS):
        piece = turn[m * width * rows : (m + 1) * width * rows, :]
        outs[m][...] = piece.astype(BF).reshape(width, rows, ri)


def projections(me, neighbors, occ, blocks, after, rows=16):
    pairs, ri = blocks.shape[2:]
    wide = occ.shape[1]
    width = wide // SLOTS
    steps = width // rows
    chunk = rows * width
    smem = pl.BlockSpec(memory_space=pltpu.SMEM)
    out = pl.pallas_call(
        functools.partial(project_kernel, width, rows),
        grid=(steps,),
        in_specs=[
            smem,
            smem,
            pl.BlockSpec((1, wide, wide), lambda s: (0, 0, 0)),
            pl.BlockSpec((1, SLOTS, chunk, ri), lambda s: (0, 0, s, 0)),
            pl.BlockSpec(memory_space=pl.ANY),
        ],
        out_specs=[pl.BlockSpec((width, rows, ri), lambda s: (0, s, 0))] * SLOTS,
        out_shape=[(pltpu.VMEM if m in (2, 3, 4, 5) else pltpu.HBM)((width, width, ri), BF) for m in range(SLOTS)],
        scratch_shapes=[pltpu.VMEM((wide, wide), BF), pltpu.VMEM((wide * rows, ri), F32)],
        compiler_params=pltpu.CompilerParams(vmem_limit_bytes=17 << 20),
        cost_estimate=pl.CostEstimate(flops=1, bytes_accessed=1, transcendentals=0),
        name="projections",
    )(me, neighbors, occ, blocks, after)
    return [each.reshape(pairs, ri) for each in out]


def contract_kernel(count, begins, has_start, *refs):
    out = refs[2 * count + has_start + (len(refs) - 2 * count - has_start - 1) // 2]
    total = refs[2 * count][...] if has_start else None
    for at, (left, right) in enumerate(zip(refs[:count], refs[count : 2 * count])):
        rows = pl.ds(begins[at], left.shape[0])
        term = lax.dot_general(left[...], right[rows, :], (((0,), (0,)), ((), ())), preferred_element_type=F32)
        total = term if total is None else total + term
    out[...] = total


def contract(lefts, rights, begins, start=None, passed=()):
    ri = rights[0].shape[1]
    count = len(lefts)
    starts = [] if start is None else [start]
    vmem = pl.BlockSpec(memory_space=pltpu.VMEM)
    anywhere = pl.BlockSpec(memory_space=pl.ANY)
    return pl.pallas_call(
        functools.partial(contract_kernel, count, begins, len(starts)),
        in_specs=[vmem] * (2 * count + len(starts)) + [anywhere] * len(passed),
        out_specs=[vmem] + [anywhere] * len(passed),
        out_shape=[pltpu.VMEM((ri, ri), F32)] + [pltpu.HBM(each.shape, each.dtype) for each in passed],
        input_output_aliases={2 * count + len(starts) + at: 1 + at for at in range(len(passed))},
        compiler_params=pltpu.CompilerParams(vmem_limit_bytes=8 << 20),
        cost_estimate=pl.CostEstimate(flops=1, bytes_accessed=1, transcendentals=0),
        name="contract",
    )(*lefts, *rights, *starts, *passed)


def rows_kernel(count, rows, slab, bases, after, me_ref, *refs):
    lefts, rights = refs[:count], refs[count : 2 * count]
    rest = refs[2 * count : 2 * count + len(bases)]
    skip = 2 * count + len(bases) + after
    skip += (len(refs) - skip - len(rows)) // 2
    outs = refs[skip : skip + len(rows)]
    chip = me_ref[0] >> 1
    height = sum(rows)
    total = jnp.zeros((height, rest[0].shape[1]), F32)
    for left, right in zip(lefts, rights):
        total += jnp.dot(left[...], right[...], preferred_element_type=F32)
    for base, (kind, first) in zip(rest, bases):
        if kind == "all":
            pieces = []
            for g in range(first, first + height // slab):
                pieces.append(base[pl.ds(pl.multiple_of((chip ^ g) * slab, slab), slab), :])
            total += jnp.concatenate(pieces, axis=0) if len(pieces) > 1 else pieces[0]
        else:
            total += base[first : first + height, :]
    at = 0
    for out, each in zip(outs, rows):
        out[...] = total[at : at + each, :]
        at += each


def contract_rows(me, lefts, rights, rows, slab, bases=(), passed=(), after=()):
    ri = bases[0][2].shape[1]
    count = len(lefts)
    vmem = pl.BlockSpec(memory_space=pltpu.VMEM)
    anywhere = pl.BlockSpec(memory_space=pl.ANY)
    kinds = tuple((kind, first) for kind, first, _ in bases)
    return pl.pallas_call(
        functools.partial(rows_kernel, count, rows, slab, kinds, len(after)),
        in_specs=[pl.BlockSpec(memory_space=pltpu.SMEM)]
        + [vmem] * (2 * count + len(bases) + len(after))
        + [anywhere] * len(passed),
        out_specs=[vmem] * len(rows) + [anywhere] * len(passed),
        out_shape=[pltpu.VMEM((each, ri), F32) for each in rows]
        + [pltpu.HBM(each.shape, each.dtype) for each in passed],
        input_output_aliases={1 + 2 * count + len(bases) + len(after) + at: len(rows) + at for at in range(len(passed))},
        compiler_params=pltpu.CompilerParams(vmem_limit_bytes=8 << 20),
        cost_estimate=pl.CostEstimate(flops=20_000_000_000, bytes_accessed=1, transcendentals=0),
        name="contract_rows",
    )(me, *lefts, *rights, *[array for _, _, array in bases], *after, *passed)


def exchange(value, k, devices):
    return lax.ppermute(value, "tensor", [(i, i ^ k) for i in range(devices)])


def reduce_rows(total, devices, order):
    index = lax.axis_index("tensor")
    bits = [1 << b for b in reversed(range(devices.bit_length() - 1))]
    value = total.reshape((2,) * len(bits) + (total.shape[0] // devices, total.shape[1]))
    left = list(bits)
    for k in order:
        at = left.index(k)
        left.pop(at)
        low = lax.index_in_dim(value, 0, at, keepdims=False)
        high = lax.index_in_dim(value, 1, at, keepdims=False)
        upper = (index & k) != 0
        value = jnp.where(upper, high, low) + exchange(jnp.where(upper, low, high), k, devices)
    return value


def local(devices, three_center, occ_green, virt_green, neighbors):
    me = lax.axis_index("tensor").astype(jnp.int32).reshape(1)
    by_slot = pltpu.with_memory_space_constraint(neighbors.T, pltpu.HBM)
    three_center = pltpu.with_memory_space_constraint(three_center, pltpu.HBM)
    occ_green = pltpu.with_memory_space_constraint(occ_green, pltpu.HBM)
    virt_green = pltpu.with_memory_space_constraint(virt_green, pltpu.HBM)
    middle, last = (2, 3, 4, 5), (6, 7)
    pairs = three_center.shape[2]
    slab = 2 * three_center.shape[-1] // devices
    by_owner = devices == 16 and slab == 16
    cuts = (((3, 8), (0, 3)), ((3, 8), (1, 3), (0, 1))) * 2 if by_owner else (((0, devices // 2),),) * 4
    begun = products(last, by_slot, virt_green, three_center, 8, near=True, wanted=((0, 0, 2), (1, 0, 2)))
    begun_in = [exchange(value, k, devices) for k, value in zip(last, begun)]
    own, *both = products(
        (0, 1) + last,
        by_slot,
        virt_green,
        three_center,
        4,
        begun[:1],
        wanted=((0, 0, 4), (1, 0, 1), (1, 1, 2), (1, 2, 3), (1, 3, 4), (2, 1, 4), (3, 1, 4)),
    )
    other, ended = both[:4], both[4:]
    ended_in = [exchange(value, k, devices) for k, value in zip(last, ended)]
    other_in = [exchange(value, 1, devices) for value in other]
    if by_owner:
        pieces = turned_products(middle, by_slot, virt_green, three_center, 4, slab, cuts, own)
        latest = pieces[5][0]
    else:
        sides = products(middle, by_slot, virt_green, three_center, 4, [own])
        arrived = {k: exchange(value, k, devices) for k, value in zip(middle, sides)}
        latest = sides[0]
    project = projections(me, by_slot, occ_green, three_center, latest)
    first, second = (4, 2), (5, 3)
    total, *passed = contract(
        [begun_in[0], own],
        [project[6], project[0]],
        (0, 0),
        None,
        [pieces[k][0] for k in second] if by_owner else [],
    )
    (total,) = contract([begun_in[1]], [project[7]], (0,), total)
    (total,) = contract(other_in, [project[1]] * 4, [at * pairs // 4 for at in range(4)], total)
    (total,) = contract(ended_in, [project[k] for k in last], (pairs // 4,) * 2, total)
    if not by_owner:
        for group in (first, second):
            (total,) = contract([arrived[k] for k in group], [project[k] for k in group], (0, 0), total)
        bits = [1 << b for b in reversed(range(devices.bit_length() - 1))]
        return reduce_rows(total, devices, bits)

    def send(values, slots):
        return [exchange(value, k, devices) for k, value in zip(slots, values)]

    first_rights = [project[k] for k in first]
    second_rights = [project[k] for k in second]
    first_far = send([pieces[k][0] for k in first], first)
    second_far = send(passed, second)
    outer, *passed = contract_rows(
        me, first_far, first_rights, (5 * slab,), slab, [("all", 3, total)], [pieces[k][1] for k in first]
    )
    first_own = send(passed, first)
    across, outer, *passed = contract_rows(
        me, second_far, second_rights, (slab, 4 * slab), slab, [("own", 0, outer)], [pieces[k][1] for k in second]
    )
    inner = exchange(outer, 8, devices)
    second_mid = send(passed, second)
    chip, rest, *passed = contract_rows(
        me, first_own, first_rights, (slab, 2 * slab), slab, [("all", 0, total)], [pieces[k][2] for k in second]
    )
    second_near = send(passed, second)
    across = exchange(across + inner[3 * slab :], 6, devices)
    square = contract_rows(
        me, second_mid, second_rights, (slab, slab), slab, [("own", 0, rest), ("own", slab, inner)]
    )
    square = [exchange(square[at], 2 * (at + 1), devices) for at in (0, 1)]
    (chip,) = contract_rows(
        me, second_near, second_rights, (slab,), slab, [("own", 0, chip), ("own", 0, inner)]
    )
    chip = chip + across + square[0] + square[1]
    half = slab // 2
    upper = (lax.axis_index("tensor") & 1) != 0
    keep = jnp.where(upper, chip[half:], chip[:half])
    return keep + exchange(jnp.where(upper, chip[:half], chip[half:]), 1, devices)


def solution(mesh):
    devices = mesh.shape["tensor"]
    in_specs = (
        P(("group", "tensor"), None, None, None),
        P("tensor", None, None),
        P("tensor", None, None),
        P(),
    )
    out_specs = P(("group", "tensor"), None)
    return jax.shard_map(
        functools.partial(local, devices), mesh=mesh, in_specs=in_specs, out_specs=out_specs, check_vma=False
    )
```

```python
import functools

import jax
import jax.numpy as jnp
from jax import lax
from jax.experimental import pallas as pl
from jax.experimental.pallas import tpu as pltpu
from jax.sharding import PartitionSpec as P

SLOTS = 8
BF = jnp.bfloat16
F32 = jnp.float32


def gathered_rows(block, first, count, width):
    columns = []
    for step in range(count):
        rows = pl.ds(pl.multiple_of(first + step * width, width), width)
        columns.append(jnp.concatenate([block[m, rows, :] for m in range(SLOTS)], axis=0))
    return jnp.concatenate(columns, axis=1)


def masked_turned(slots, width, me, neighbors_ref, virt, virt_t):
    for pair in range(len(slots) // 2):
        parts = [
            jnp.where(neighbors_ref[m, me] >= 0, virt[pair, m * width : (m + 1) * width, :].astype(F32), 0.0)
            for m in range(SLOTS)
        ]
        turned = jnp.concatenate(parts, axis=0).T
        for at in range(2):
            live = neighbors_ref[slots[2 * pair + at], me] >= 0
            virt_t[(2 * pair + at) * width : (2 * pair + at + 1) * width, :] = jnp.where(
                live, turned[at * width : (at + 1) * width, :], 0.0
            ).astype(BF)


def virt_copies(slots, width, virt_hbm, virt, sems):
    return [
        pltpu.make_async_copy(
            virt_hbm.at[0, :, pl.ds(k * width, 2 * width)], virt.at[pair], sems.at[pair]
        )
        for pair, k in enumerate(slots[::2])
    ]


def product_kernel(slots, wanted, width, chunks, neighbors_hbm, virt_hbm, block_hbm, *refs):
    outs = refs[-7 - len(wanted) : -7]
    neighbors_ref, virt, virt_t, block, neighbors_sem, virt_sems, sems = refs[-7:]
    me = lax.axis_index("tensor")
    ri = block.shape[-1]
    size = block_hbm.shape[2] // chunks
    start = min(first for _, first, _ in wanted)
    stop = max(last for _, _, last in wanted)

    def block_copy(c):
        rows = pl.ds(pl.multiple_of((c - start) * size, size), size)
        source = pl.ds(pl.multiple_of(c * size, size), size)
        return pltpu.make_async_copy(block_hbm.at[0, :, source, :], block.at[:, rows, :], sems.at[c - start])

    neighbors_copy = pltpu.make_async_copy(neighbors_hbm, neighbors_ref, neighbors_sem)
    neighbors_copy.start()
    copies = virt_copies(slots, width, virt_hbm, virt, virt_sems)
    for copy in copies:
        copy.start()
    for c in range(start, stop):
        block_copy(c).start()
    neighbors_copy.wait()
    for copy in copies:
        copy.wait()
    masked_turned(slots, width, me, neighbors_ref, virt, virt_t)

    def run(begin, end, busy):
        low = min(wanted[at][0] for at in busy) * width
        high = (max(wanted[at][0] for at in busy) + 1) * width

        @pl.loop(begin, end)
        def _(c):
            block_copy(c).wait()
            for pair in range(size // width // 2):
                inner = 2 * pair * width
                right = gathered_rows(block, (c - start) * size + inner, 2, width)
                both = jnp.dot(virt_t[low:high, :], right, preferred_element_type=F32).astype(BF)
                for at in busy:
                    row = wanted[at][0] * width - low
                    for half in range(2):
                        base = (c - wanted[at][1]) * size + inner + half * width
                        rows = pl.ds(pl.multiple_of(base, width), width)
                        outs[at][rows, :] = both[row : row + width, half * ri : (half + 1) * ri]

    edges = sorted({edge for _, *each in wanted for edge in each})
    for begin, end in zip(edges, edges[1:]):
        run(begin, end, [at for at, (_, first, last) in enumerate(wanted) if first <= begin and end <= last])


def products(slots, neighbors, virt, blocks, chunks, after=(), near=False, wanted=None):
    pairs, ri = blocks.shape[2:]
    wide = virt.shape[1]
    width = wide // SLOTS
    count = len(slots)
    wanted = wanted or tuple((at, 0, chunks) for at in range(count))
    used = max(last for _, _, last in wanted) - min(first for _, first, _ in wanted)
    shapes = [(pairs // chunks * (last - first), ri) for _, first, last in wanted]
    hbm = pl.BlockSpec(memory_space=pltpu.HBM)
    return pl.pallas_call(
        functools.partial(product_kernel, slots, wanted, width, chunks),
        in_specs=[hbm, hbm, hbm] + [pl.BlockSpec(memory_space=pl.ANY)] * len(after),
        out_specs=[pl.BlockSpec(memory_space=pltpu.VMEM)] * len(wanted),
        out_shape=[(pltpu.VMEM if near else pltpu.HBM)(shape, BF) for shape in shapes],
        scratch_shapes=[
            pltpu.SMEM(neighbors.shape, jnp.int32),
            pltpu.VMEM((count // 2, wide, 2 * width), BF),
            pltpu.VMEM((count * width, wide), BF),
            pltpu.VMEM((SLOTS, pairs // chunks * used, ri), BF),
            pltpu.SemaphoreType.DMA,
            pltpu.SemaphoreType.DMA((count // 2,)),
            pltpu.SemaphoreType.DMA((used,)),
        ],
        compiler_params=pltpu.CompilerParams(vmem_limit_bytes=24 << 20),
        cost_estimate=pl.CostEstimate(flops=1, bytes_accessed=1, transcendentals=0),
        name="products",
    )(neighbors, virt, blocks, *after)


def turned_product_kernel(slots, width, chunks, slab, cuts, neighbors_hbm, virt_hbm, block_hbm, *refs):
    count = len(slots)
    pieces = sum(len(each) for each in cuts)
    outs = refs[-9 - pieces : -9]
    neighbors_ref, virt, virt_t, block, sides, neighbors_sem, virt_sems, sems, out_sems = refs[-9:]
    me = lax.axis_index("tensor")
    ri = block.shape[-1]
    size = block.shape[1] // chunks

    def block_copy(c):
        rows = pl.ds(pl.multiple_of(c * size, size), size)
        return pltpu.make_async_copy(block_hbm.at[0, :, rows, :], block.at[:, rows, :], sems.at[c])

    neighbors_copy = pltpu.make_async_copy(neighbors_hbm, neighbors_ref, neighbors_sem)
    neighbors_copy.start()
    virt_moves = virt_copies(slots, width, virt_hbm, virt, virt_sems)
    for copy in virt_moves:
        copy.start()
    for c in range(chunks):
        block_copy(c).start()
    neighbors_copy.wait()
    for copy in virt_moves:
        copy.wait()
    masked_turned(slots, width, me, neighbors_ref, virt, virt_t)

    @pl.loop(0, chunks)
    def _(c):
        block_copy(c).wait()
        for pair in range(size // width // 2):
            base = c * size + 2 * pair * width
            right = gathered_rows(block, base, 2, width)
            both = jnp.dot(virt_t[...], right, preferred_element_type=F32).astype(BF)
            lanes = pl.ds(pl.multiple_of(base, 2 * width), 2 * width)
            for at in range(count):
                mine = both[at * width : (at + 1) * width, :]
                rows = jnp.concatenate([mine[:, :ri], mine[:, ri:]], axis=0)
                sides[at, :, lanes] = rows.T

    copies = []
    outs = list(outs)
    for at, k in enumerate(slots):
        chip = (me ^ k) >> 1
        for first, last in cuts[at]:
            out = outs.pop(0)
            for g in range(first, last):
                source = pl.ds(pl.multiple_of((chip ^ g) * slab, slab), slab)
                target = out.at[pl.ds((g - first) * slab, slab), :]
                copies.append(pltpu.make_async_copy(sides.at[at, source, :], target, out_sems.at[len(copies)]))
    for copy in copies:
        copy.start()
    for copy in copies:
        copy.wait()


def turned_products(slots, neighbors, virt, blocks, chunks, slab, cuts, after):
    pairs, ri = blocks.shape[2:]
    wide = virt.shape[1]
    width = wide // SLOTS
    count = len(slots)
    hbm = pl.BlockSpec(memory_space=pltpu.HBM)
    out = pl.pallas_call(
        functools.partial(turned_product_kernel, slots, width, chunks, slab, cuts),
        in_specs=[hbm, hbm, hbm, pl.BlockSpec(memory_space=pl.ANY)],
        out_specs=[hbm] * sum(len(each) for each in cuts),
        out_shape=[pltpu.HBM(((last - first) * slab, pairs), BF) for each in cuts for first, last in each],
        scratch_shapes=[
            pltpu.SMEM(neighbors.shape, jnp.int32),
            pltpu.VMEM((count // 2, wide, 2 * width), BF),
            pltpu.VMEM((count * width, wide), BF),
            pltpu.VMEM((SLOTS, pairs, ri), BF),
            pltpu.VMEM((count, ri, pairs), BF),
            pltpu.SemaphoreType.DMA,
            pltpu.SemaphoreType.DMA((count // 2,)),
            pltpu.SemaphoreType.DMA((chunks,)),
            pltpu.SemaphoreType.DMA((count * ri // slab,)),
        ],
        compiler_params=pltpu.CompilerParams(vmem_limit_bytes=24 << 20),
        cost_estimate=pl.CostEstimate(flops=1, bytes_accessed=1, transcendentals=0),
        name="turned_products",
    )(neighbors, virt, blocks, after)
    out = list(out)
    return {k: [out.pop(0) for _ in cuts[at]] for at, k in enumerate(slots)}


def project_kernel(width, rows, me_ref, neighbors_ref, occ_ref, block_ref, after_ref, *refs):
    outs, occ, turn = refs[:-2], refs[-2], refs[-1]
    me = me_ref[0]
    wide = SLOTS * width

    @pl.when(pl.program_id(0) == 0)
    def _():
        slot = lax.broadcasted_iota(jnp.int32, (1, wide), 1) // width
        keep = jnp.zeros((1, wide), F32)
        for n in range(SLOTS):
            keep = jnp.where((slot == n) & (neighbors_ref[n, me] >= 0), 1.0, keep)
        occ[...] = (occ_ref[0].astype(F32) * keep).astype(BF)

    ri = block_ref.shape[-1]
    for pair in range(rows // 2):
        right = gathered_rows(block_ref.at[0], 2 * pair * width, 2, width)
        both = jnp.dot(occ[...], right, preferred_element_type=F32)
        for half in range(2):
            turn[pl.ds(2 * pair + half, wide, stride=rows), :] = both[:, half * ri : (half + 1) * ri]
    for m in range(SLOTS):
        piece = turn[m * width * rows : (m + 1) * width * rows, :]
        outs[m][...] = piece.astype(BF).reshape(width, rows, ri)


def projections(me, neighbors, occ, blocks, after, rows=16):
    pairs, ri = blocks.shape[2:]
    wide = occ.shape[1]
    width = wide // SLOTS
    steps = width // rows
    chunk = rows * width
    smem = pl.BlockSpec(memory_space=pltpu.SMEM)
    out = pl.pallas_call(
        functools.partial(project_kernel, width, rows),
        grid=(steps,),
        in_specs=[
            smem,
            smem,
            pl.BlockSpec((1, wide, wide), lambda s: (0, 0, 0)),
            pl.BlockSpec((1, SLOTS, chunk, ri), lambda s: (0, 0, s, 0)),
            pl.BlockSpec(memory_space=pl.ANY),
        ],
        out_specs=[pl.BlockSpec((width, rows, ri), lambda s: (0, s, 0))] * SLOTS,
        out_shape=[(pltpu.VMEM if m in (2, 3, 4, 5) else pltpu.HBM)((width, width, ri), BF) for m in range(SLOTS)],
        scratch_shapes=[pltpu.VMEM((wide, wide), BF), pltpu.VMEM((wide * rows, ri), F32)],
        compiler_params=pltpu.CompilerParams(vmem_limit_bytes=17 << 20),
        cost_estimate=pl.CostEstimate(flops=1, bytes_accessed=1, transcendentals=0),
        name="projections",
    )(me, neighbors, occ, blocks, after)
    return [each.reshape(pairs, ri) for each in out]


def contract_kernel(count, begins, has_start, *refs):
    out = refs[2 * count + has_start + (len(refs) - 2 * count - has_start - 1) // 2]
    total = refs[2 * count][...] if has_start else None
    for at, (left, right) in enumerate(zip(refs[:count], refs[count : 2 * count])):
        rows = pl.ds(begins[at], left.shape[0])
        term = lax.dot_general(left[...], right[rows, :], (((0,), (0,)), ((), ())), preferred_element_type=F32)
        total = term if total is None else total + term
    out[...] = total


def contract(lefts, rights, begins, start=None, passed=()):
    ri = rights[0].shape[1]
    count = len(lefts)
    starts = [] if start is None else [start]
    vmem = pl.BlockSpec(memory_space=pltpu.VMEM)
    anywhere = pl.BlockSpec(memory_space=pl.ANY)
    return pl.pallas_call(
        functools.partial(contract_kernel, count, begins, len(starts)),
        in_specs=[vmem] * (2 * count + len(starts)) + [anywhere] * len(passed),
        out_specs=[vmem] + [anywhere] * len(passed),
        out_shape=[pltpu.VMEM((ri, ri), F32)] + [pltpu.HBM(each.shape, each.dtype) for each in passed],
        input_output_aliases={2 * count + len(starts) + at: 1 + at for at in range(len(passed))},
        compiler_params=pltpu.CompilerParams(vmem_limit_bytes=8 << 20),
        cost_estimate=pl.CostEstimate(flops=1, bytes_accessed=1, transcendentals=0),
        name="contract",
    )(*lefts, *rights, *starts, *passed)


def rows_kernel(count, rows, slab, bases, after, me_ref, *refs):
    lefts, rights = refs[:count], refs[count : 2 * count]
    rest = refs[2 * count : 2 * count + len(bases)]
    skip = 2 * count + len(bases) + after
    skip += (len(refs) - skip - len(rows)) // 2
    outs = refs[skip : skip + len(rows)]
    chip = me_ref[0] >> 1
    height = sum(rows)
    total = jnp.zeros((height, rest[0].shape[1]), F32)
    for left, right in zip(lefts, rights):
        total += jnp.dot(left[...], right[...], preferred_element_type=F32)
    for base, (kind, first) in zip(rest, bases):
        if kind == "all":
            pieces = []
            for g in range(first, first + height // slab):
                pieces.append(base[pl.ds(pl.multiple_of((chip ^ g) * slab, slab), slab), :])
            total += jnp.concatenate(pieces, axis=0) if len(pieces) > 1 else pieces[0]
        else:
            total += base[first : first + height, :]
    at = 0
    for out, each in zip(outs, rows):
        out[...] = total[at : at + each, :]
        at += each


def contract_rows(me, lefts, rights, rows, slab, bases=(), passed=(), after=()):
    ri = bases[0][2].shape[1]
    count = len(lefts)
    vmem = pl.BlockSpec(memory_space=pltpu.VMEM)
    anywhere = pl.BlockSpec(memory_space=pl.ANY)
    kinds = tuple((kind, first) for kind, first, _ in bases)
    return pl.pallas_call(
        functools.partial(rows_kernel, count, rows, slab, kinds, len(after)),
        in_specs=[pl.BlockSpec(memory_space=pltpu.SMEM)]
        + [vmem] * (2 * count + len(bases) + len(after))
        + [anywhere] * len(passed),
        out_specs=[vmem] * len(rows) + [anywhere] * len(passed),
        out_shape=[pltpu.VMEM((each, ri), F32) for each in rows]
        + [pltpu.HBM(each.shape, each.dtype) for each in passed],
        input_output_aliases={1 + 2 * count + len(bases) + len(after) + at: len(rows) + at for at in range(len(passed))},
        compiler_params=pltpu.CompilerParams(vmem_limit_bytes=8 << 20),
        cost_estimate=pl.CostEstimate(flops=20_000_000_000, bytes_accessed=1, transcendentals=0),
        name="contract_rows",
    )(me, *lefts, *rights, *[array for _, _, array in bases], *after, *passed)


def exchange(value, k, devices):
    return lax.ppermute(value, "tensor", [(i, i ^ k) for i in range(devices)])


def reduce_rows(total, devices, order):
    index = lax.axis_index("tensor")
    bits = [1 << b for b in reversed(range(devices.bit_length() - 1))]
    value = total.reshape((2,) * len(bits) + (total.shape[0] // devices, total.shape[1]))
    left = list(bits)
    for k in order:
        at = left.index(k)
        left.pop(at)
        low = lax.index_in_dim(value, 0, at, keepdims=False)
        high = lax.index_in_dim(value, 1, at, keepdims=False)
        upper = (index & k) != 0
        value = jnp.where(upper, high, low) + exchange(jnp.where(upper, low, high), k, devices)
    return value


def local(devices, three_center, occ_green, virt_green, neighbors):
    me = lax.axis_index("tensor").astype(jnp.int32).reshape(1)
    by_slot = pltpu.with_memory_space_constraint(neighbors.T, pltpu.HBM)
    three_center = pltpu.with_memory_space_constraint(three_center, pltpu.HBM)
    occ_green = pltpu.with_memory_space_constraint(occ_green, pltpu.HBM)
    virt_green = pltpu.with_memory_space_constraint(virt_green, pltpu.HBM)
    middle, last = (2, 3, 4, 5), (6, 7)
    pairs = three_center.shape[2]
    slab = 2 * three_center.shape[-1] // devices
    by_owner = devices == 16 and slab == 16
    cuts = (((3, 8), (0, 3)), ((3, 8), (1, 3), (0, 1))) * 2 if by_owner else (((0, devices // 2),),) * 4
    begun = products(last, by_slot, virt_green, three_center, 8, near=True, wanted=((0, 0, 2), (1, 0, 2)))
    begun_in = [exchange(value, k, devices) for k, value in zip(last, begun)]
    own, *both = products(
        (0, 1) + last,
        by_slot,
        virt_green,
        three_center,
        4,
        begun[:1],
        wanted=((0, 0, 4), (1, 0, 1), (1, 1, 2), (1, 2, 3), (1, 3, 4), (2, 1, 4), (3, 1, 4)),
    )
    other, ended = both[:4], both[4:]
    ended_in = [exchange(value, k, devices) for k, value in zip(last, ended)]
    other_in = [exchange(value, 1, devices) for value in other]
    if by_owner:
        pieces = turned_products(middle, by_slot, virt_green, three_center, 4, slab, cuts, own)
        latest = pieces[5][0]
    else:
        sides = products(middle, by_slot, virt_green, three_center, 4, [own])
        arrived = {k: exchange(value, k, devices) for k, value in zip(middle, sides)}
        latest = sides[0]
    project = projections(me, by_slot, occ_green, three_center, latest)
    first, second = (4, 2), (5, 3)
    total, *passed = contract(
        [begun_in[0], own],
        [project[6], project[0]],
        (0, 0),
        None,
        [pieces[k][0] for k in second] if by_owner else [],
    )
    (total,) = contract([begun_in[1]], [project[7]], (0,), total)
    (total,) = contract(other_in, [project[1]] * 4, [at * pairs // 4 for at in range(4)], total)
    (total,) = contract(ended_in, [project[k] for k in last], (pairs // 4,) * 2, total)
    if not by_owner:
        for group in (first, second):
            (total,) = contract([arrived[k] for k in group], [project[k] for k in group], (0, 0), total)
        bits = [1 << b for b in reversed(range(devices.bit_length() - 1))]
        return reduce_rows(total, devices, bits)

    def send(values, slots):
        return [exchange(value, k, devices) for k, value in zip(slots, values)]

    first_rights = [project[k] for k in first]
    second_rights = [project[k] for k in second]
    first_far = send([pieces[k][0] for k in first], first)
    second_far = send(passed, second)
    outer, *passed = contract_rows(
        me, first_far, first_rights, (5 * slab,), slab, [("all", 3, total)], [pieces[k][1] for k in first]
    )
    first_own = send(passed, first)
    across, outer, *passed = contract_rows(
        me, second_far, second_rights, (slab, 4 * slab), slab, [("own", 0, outer)], [pieces[k][1] for k in second]
    )
    inner = exchange(outer, 8, devices)
    second_mid = send(passed, second)
    chip, rest, *passed = contract_rows(
        me, first_own, first_rights, (slab, 2 * slab), slab, [("all", 0, total)], [pieces[k][2] for k in second]
    )
    second_near = send(passed, second)
    (across,) = contract_rows(
        me, [], [], (slab,), slab, [("own", 0, across), ("own", 3 * slab, inner)], (), [rest]
    )
    across = exchange(across, 6, devices)
    square = contract_rows(
        me, second_mid, second_rights, (slab, slab), slab, [("own", 0, rest), ("own", slab, inner)]
    )
    square = [exchange(square[at], 2 * (at + 1), devices) for at in (0, 1)]
    (chip,) = contract_rows(
        me, second_near, second_rights, (slab,), slab, [("own", 0, chip), ("own", 0, inner)]
    )
    chip = chip + across + square[0] + square[1]
    half = slab // 2
    upper = (lax.axis_index("tensor") & 1) != 0
    keep = jnp.where(upper, chip[half:], chip[:half])
    return keep + exchange(jnp.where(upper, chip[:half], chip[half:]), 1, devices)


def solution(mesh):
    devices = mesh.shape["tensor"]
    in_specs = (
        P(("group", "tensor"), None, None, None),
        P("tensor", None, None),
        P("tensor", None, None),
        P(),
    )
    out_specs = P(("group", "tensor"), None)
    return jax.shard_map(
        functools.partial(local, devices), mesh=mesh, in_specs=in_specs, out_specs=out_specs, check_vma=False
    )
```
